32 devices in a mesh: wide: 4 (over y, x), narrow: 8 (over z, core).
Axes of the slice: x: 2, y: 2, z: 4, core: 2. Of those that a mesh axis runs over, the one named last changes fastest.
Arguments:
- features: bfloat16 [65536, 128], P(('wide', 'narrow')), may hold values from -6 to 6
- band_tiles: int32 [512, 8, 128, 128], P(('wide', 'narrow')), may hold values 0 or 1
- band_cols: int32 [512, 8], P(('wide', 'narrow')), may hold values from 0 to 15
- off_tiles: int32 [32, 4, 128, 128], P(('wide', 'narrow')), may hold values 0 or 1
- req_block: int32 [32, 4], P(('wide', 'narrow')), may hold values from 0 to 15
- req_row: int32 [32, 4], P(('wide', 'narrow')), may hold values from 0 to 15
- req_valid: int32 [32, 4], P(('wide', 'narrow')), may hold values 0 or 1
- weight_self: bfloat16 [128, 256], replicated, may hold values from -0.5 to 0.5
- weight_neigh: bfloat16 [128, 256], replicated, may hold values from -1.5 to 1.5
- bias_term: bfloat16 [256], replicated, may hold values from -3 to 3
- cotangent: bfloat16 [65536, 256], P(('wide', 'narrow')), may hold values from -6 to 6
Outputs:
- layer_out: bfloat16 [65536, 256], P(('wide', 'narrow'))
- grad_features: float32 [65536, 128], P(('wide', 'narrow'))
- grad_self: float32 [128, 256], replicated
- grad_neigh: float32 [128, 256], replicated
- grad_bias: float32 [256], replicated
The draws below stay inside these ranges and needn't reach their ends.
All inputs are finite; a program needn't handle non-finite values. No bound on the sum of `band_tiles` or of `off_tiles` or of `req_valid` on one device may be relied on, other than what follows from the above.
Results may differ from the reference program's by a relative error of at most 0.007.
Values may be sent and summed in bfloat16 or wider, within the bound.
No kernel may reach another device: no remote copies, remote signals or barrier semaphores. Data moves between devices by JAX's collectives and lax.ppermute only.
A program may use at most 128 MiB of HBM per device.

```python
import jax
import jax.numpy as jnp
from jax import lax

F_IN = 128
F_OUT = 256
BLOCK = 128
BLK_DEV = 16
NBLOCKS = 512
NODES = 65536
N_WIDE = 4
N_NARROW = 8
DEVICES = 32


def set_ends(result, key, least, high):
    dims = result.shape
    place = [jax.random.randint(jax.random.fold_in(key, axis), (), 0, dims[axis]) for axis in range(len(dims))]
    result = result.at[tuple(place)].set(least)
    longest = dims.index(max(dims))
    place[longest] = (place[longest] + 1) % dims[longest]
    return result.at[tuple(place)].set(high)


def block_levels(stream_key, shape, shards, low, high):
    gain = 1.0
    for axis_at, parts in shards:
        steps = jax.random.uniform(jax.random.fold_in(jax.random.fold_in(stream_key, 6), axis_at), (parts,), jnp.float32, low / len(shards), high / len(shards))
        gain = gain * jnp.repeat(jnp.exp(steps), shape[axis_at] // parts).reshape((-1,) + (1,) * (len(shape) - 1 - axis_at))
    return gain


def scatter_about(rng, shape, scale, reach, split=(), kind=jnp.bfloat16):
    array = scale * jax.random.normal(rng, shape, jnp.float32)
    if split:
        array = array * block_levels(rng, shape, split, -0.22, 0.18)
    return jnp.clip(array, -reach, reach).astype(kind)


def setup_inputs(seed: int = 0) -> dict:
    arg_keys = jax.random.split(jax.random.key(seed), 12)
    return {
        "features": scatter_about(arg_keys[0], (NODES, F_IN), 1.0, 6.0, ((0, 32),)),
        "band_tiles": set_ends((jax.random.randint(arg_keys[1], (NBLOCKS, N_NARROW, BLOCK, BLOCK), 0, 64) < 1).astype(jnp.int32), jax.random.fold_in(arg_keys[1], 1), 0, 1),
        "band_cols": set_ends(jax.random.randint(arg_keys[2], (NBLOCKS, N_NARROW), 0, BLK_DEV), jax.random.fold_in(arg_keys[2], 1), 0, BLK_DEV - 1).astype(jnp.int32),
        "off_tiles": set_ends((jax.random.randint(arg_keys[3], (DEVICES, N_WIDE, BLOCK, BLOCK), 0, 8) < 1).astype(jnp.int32), jax.random.fold_in(arg_keys[3], 1), 0, 1),
        "req_block": set_ends(jax.random.randint(arg_keys[4], (DEVICES, N_WIDE), 0, BLK_DEV), jax.random.fold_in(arg_keys[4], 1), 0, BLK_DEV - 1).astype(jnp.int32),
        "req_row": set_ends(jax.random.randint(arg_keys[5], (DEVICES, N_WIDE), 0, BLK_DEV), jax.random.fold_in(arg_keys[5], 1), 0, BLK_DEV - 1).astype(jnp.int32),
        "req_valid": set_ends((jax.random.randint(arg_keys[6], (DEVICES, N_WIDE), 0, 4) < 3).astype(jnp.int32), jax.random.fold_in(arg_keys[6], 1), 0, 1),
        "weight_self": scatter_about(arg_keys[7], (F_IN, F_OUT), F_IN ** -0.5, 0.5),
        "weight_neigh": scatter_about(arg_keys[8], (F_IN, F_OUT), (F_IN // 8) ** -0.5, 1.5),
        "bias_term": scatter_about(arg_keys[9], (F_OUT,), 0.5, 3.0),
        "cotangent": scatter_about(arg_keys[10], (NODES, F_OUT), 1.0, 6.0, ((0, 32),)),
    }


def reference(features, band_tiles, band_cols, off_tiles, req_block, req_row, req_valid, weight_self, weight_neigh, bias_term, cotangent):
    feat_blocks = features.reshape(NBLOCKS, BLOCK, F_IN)
    block_ids = jnp.arange(NBLOCKS, dtype=jnp.int32)
    group_base = block_ids // BLK_DEV // N_NARROW * N_NARROW
    slab_ids = jnp.arange(N_NARROW, dtype=jnp.int32)

    def band_sum(totals, which):
        target = (group_base + which) * BLK_DEV + band_cols[:, which]
        tile = band_tiles[:, which].astype(jnp.float32)
        picked = feat_blocks[target].astype(jnp.float32)
        return (totals + jnp.einsum('gij,gjf->gif', tile, picked), None)
    gathered, _ = lax.scan(band_sum, jnp.zeros((NBLOCKS, BLOCK, F_IN), jnp.float32), slab_ids)
    degree = lax.optimization_barrier(jnp.sum(band_tiles.astype(jnp.float32), axis=(1, 3)))
    device_ids = jnp.arange(DEVICES, dtype=jnp.int32)[:, None]
    source = (jnp.arange(N_WIDE, dtype=jnp.int32)[None, :] * N_NARROW + device_ids % N_NARROW) * BLK_DEV + req_block
    target = device_ids * BLK_DEV + req_row
    masked = off_tiles.astype(jnp.float32) * req_valid.astype(jnp.float32)[:, :, None, None]
    pulled = jnp.einsum('dwij,dwjf->dwif', masked, feat_blocks[source].astype(jnp.float32))
    flat_target = target.reshape(-1)
    flat_source = source.reshape(-1)
    gathered = gathered.at[flat_target].add(pulled.reshape(-1, BLOCK, F_IN))
    degree = degree.at[flat_target].add(lax.optimization_barrier(jnp.sum(masked, axis=3)).reshape(-1, BLOCK))
    denom = degree + 1.0
    aggregate = (gathered / denom[:, :, None]).reshape(NODES, F_IN).astype(jnp.bfloat16)
    pre = jnp.dot(features, weight_self, preferred_element_type=jnp.float32)
    pre = pre + jnp.dot(aggregate, weight_neigh, preferred_element_type=jnp.float32) + bias_term.astype(jnp.float32)
    activated, pullback = jax.vjp(lambda value: jax.nn.gelu(value, approximate=True), pre)
    layer_out = activated.astype(jnp.bfloat16)
    grad_pre = pullback(cotangent.astype(jnp.float32))[0].astype(jnp.bfloat16)
    factor = NODES ** (-0.5)
    grad_self = jnp.dot(features.T, grad_pre, preferred_element_type=jnp.float32) * factor
    grad_neigh = jnp.dot(aggregate.T, grad_pre, preferred_element_type=jnp.float32) * factor
    grad_bias = lax.optimization_barrier(jnp.sum(grad_pre.astype(jnp.float32), axis=0)) * factor
    grad_agg = jnp.dot(grad_pre, weight_neigh.T, preferred_element_type=jnp.float32)
    signal = (grad_agg.reshape(NBLOCKS, BLOCK, F_IN) / denom[:, :, None]).astype(jnp.bfloat16)
    signal_wide = signal.astype(jnp.float32)
    local_ids = jnp.arange(BLK_DEV, dtype=jnp.int32)
    device_base = jnp.arange(DEVICES, dtype=jnp.int32) // N_NARROW * N_NARROW

    def band_back(totals, which):
        tile = band_tiles[:, which].astype(jnp.float32)
        moved = jnp.einsum('gji,gjf->gif', tile, signal_wide).reshape(DEVICES, BLK_DEV, BLOCK, F_IN)
        columns = band_cols[:, which].reshape(DEVICES, BLK_DEV)
        one_hot = (columns[:, :, None] == local_ids[None, None, :]).astype(jnp.float32)
        term = jnp.einsum('ebt,ebif->etif', one_hot, moved, precision=lax.Precision.HIGHEST)
        term = lax.optimization_barrier(term.astype(jnp.bfloat16)).astype(jnp.float32)
        dest = ((device_base + which)[:, None] * BLK_DEV + local_ids[None, :]).reshape(-1)
        return (totals.at[dest].add(term.reshape(-1, BLOCK, F_IN)), None)
    returned, _ = lax.scan(band_back, jnp.zeros((NBLOCKS, BLOCK, F_IN), jnp.float32), slab_ids)
    pushed = jnp.einsum('dwji,dwjf->dwif', masked, signal_wide[target])
    pushed = lax.optimization_barrier(pushed.astype(jnp.bfloat16)).astype(jnp.float32)
    returned = returned.at[flat_source].add(pushed.reshape(-1, BLOCK, F_IN))
    grad_features = jnp.dot(grad_pre, weight_self.T, preferred_element_type=jnp.float32) + returned.reshape(NODES, F_IN)
    return (layer_out, grad_features, grad_self, grad_neigh, grad_bias)
```

```python
from functools import partial

import jax
import jax.numpy as jnp
from jax import lax
from jax.experimental import pallas as pl
from jax.experimental.pallas import tpu as pltpu
from jax.sharding import PartitionSpec as P

F32 = jnp.float32
BF16 = jnp.bfloat16
BLK = 128
ROWS_PER = 4
VMEM = 48 * 1024 * 1024


def mm(a, b, lhs=1, rhs=0):
    return lax.dot_general(a, b, (((lhs,), (rhs,)), ((), ())), preferred_element_type=F32)


def params():
    return pltpu.CompilerParams(vmem_limit_bytes=VMEM)


def cost(flops, nbytes, trans=0):
    return pl.CostEstimate(flops=flops, bytes_accessed=nbytes, transcendentals=trans)


def prep_kernel(t_ref, plain_ref, turned_ref, deg_ref):
    total = jnp.zeros((BLK, BLK), F32)
    for k in range(t_ref.shape[1]):
        t = t_ref[0, k].astype(F32)
        total = total + t
        plain_ref[0, k] = t.astype(BF16)
        turned_ref[0, k] = t.T.astype(BF16)
    deg_ref[...] = jnp.broadcast_to(jnp.sum(total, axis=1, keepdims=True), (BLK, BLK))


def prep(tiles):
    g, n = tiles.shape[:2]
    tile_spec = pl.BlockSpec((1, n, BLK, BLK), lambda i: (i, 0, 0, 0))
    return pl.pallas_call(
        prep_kernel,
        grid=(g,),
        in_specs=[tile_spec],
        out_specs=[tile_spec, tile_spec, pl.BlockSpec((BLK, BLK), lambda i: (i, 0))],
        out_shape=[
            jax.ShapeDtypeStruct(tiles.shape, BF16),
            jax.ShapeDtypeStruct(tiles.shape, BF16),
            jax.ShapeDtypeStruct((g * BLK, BLK), F32),
        ],
        compiler_params=params(),
        cost_estimate=cost(tiles.size, tiles.size * 8),
        name="prep",
    )(tiles)


def block(ref, index):
    return ref[pl.ds(pl.multiple_of(index * BLK, BLK), BLK), :]


def pull_sum(ids, cols, tiles_ref, own_ref, sib_ref, b, g, n, step):
    core, chip = ids[0], ids[1 + step]
    own = block(own_ref, cols[g * n + chip * 2 + core])
    sib = block(sib_ref, cols[g * n + chip * 2 + 1 - core])
    return mm(tiles_ref[b, core], own) + mm(tiles_ref[b, 1 - core], sib)


def pull_kernel(ids, cols, *refs, n, step, first):
    if first:
        tiles_ref, own_ref, sib_ref, out_ref = refs
    else:
        tiles_ref, own_ref, sib_ref, acc_ref, out_ref = refs
    i = pl.program_id(0)
    for b in range(ROWS_PER):
        rows = pl.ds(b * BLK, BLK)
        part = pull_sum(ids, cols, tiles_ref, own_ref, sib_ref, b, i * ROWS_PER + b, n, step)
        out_ref[rows, :] = part if first else acc_ref[rows, :] + part


def pull(ids, cols, tiles, own, sib, acc, step):
    g, n = tiles.shape[:2]
    rows, width = own.shape
    whole = pl.BlockSpec((rows, width), lambda i, ids, cols: (0, 0))
    part = pl.BlockSpec((ROWS_PER * BLK, width), lambda i, ids, cols: (i, 0))
    pair = pl.BlockSpec((ROWS_PER, 2, BLK, BLK), lambda i, ids, cols: (i, ids[1 + step], 0, 0))
    more = () if acc is None else (acc,)
    return pl.pallas_call(
        partial(pull_kernel, n=n, step=step, first=acc is None),
        grid_spec=pltpu.PrefetchScalarGridSpec(
            num_scalar_prefetch=2,
            grid=(g // ROWS_PER,),
            in_specs=[pair, whole, whole] + [part] * len(more),
            out_specs=part,
        ),
        out_shape=jax.ShapeDtypeStruct((rows, width), F32),
        compiler_params=params(),
        cost_estimate=cost(4 * rows * BLK * width, 12 * rows * width),
        name=f"pull{step}",
    )(ids, cols, tiles, own, sib, *more)


def off_kernel(asked, row, valid, off_ref, *refs, wide):
    fetched, (acc_in, deg_in, acc_ref, deg_ref) = refs[:wide], refs[wide:]
    acc_ref[...] = acc_in[...]
    deg_ref[...] = deg_in[...]
    here = lax.axis_index("wide")
    for k in range(wide):
        src = source(here, k, wide)
        mask = off_ref[0, src].astype(F32) * valid[src].astype(F32)
        at = pl.ds(pl.multiple_of(row[src] * BLK, BLK), BLK)
        acc_ref[at, :] += mm(mask.astype(BF16), fetched[k][...])
        deg_ref[at, :] += jnp.broadcast_to(jnp.sum(mask, axis=1, keepdims=True), (BLK, BLK))


def off_band(asked, row, valid, off_tiles, by_peer, acc, deg):
    wide = len(by_peer)
    rows, width = acc.shape

    def spec_of(k):
        return pl.BlockSpec(
            (BLK, width), lambda i, asked, row, valid: (asked[wide + k], 0)
        )

    full = pl.BlockSpec((rows, width), lambda i, *s: (0, 0))
    offs = pl.BlockSpec(off_tiles.shape, lambda i, *s: (0, 0, 0, 0))
    return pl.pallas_call(
        partial(off_kernel, wide=wide),
        grid_spec=pltpu.PrefetchScalarGridSpec(
            num_scalar_prefetch=3,
            grid=(1,),
            in_specs=[offs] + [spec_of(k) for k in range(wide)] + [full, full],
            out_specs=[full, full],
        ),
        out_shape=[jax.ShapeDtypeStruct((rows, width), F32)] * 2,
        compiler_params=params(),
        cost_estimate=cost(2 * wide * BLK**3, 16 * rows * width),
        name="off_band",
    )(asked, row, valid, off_tiles, *by_peer, acc, deg)


def place(cols, turned, signal_rows, place_ref, g, core, chip, n):
    for j in range(2):
        which = core if j == 0 else 1 - core
        at = pl.ds(pl.multiple_of(cols[g * n + chip * 2 + which] * BLK, BLK), BLK)
        place_ref[j, at, :] += mm(turned(which), signal_rows)


def middle_kernel(
    ids, cols, tiles_ref, own_ref, sib_ref, acc_ref, deg_ref, feat_ref, cot_ref,
    wself_ref, wneigh_ref, bias_ref, turned_ref,
    out_ref, gp_ref, agg_ref, sig_ref, keep_ref, send_ref, place_ref, *, n, steps,
):
    i = pl.program_id(0)

    @pl.when(i == 0)
    def _():
        place_ref[...] = jnp.zeros_like(place_ref)

    inverse = 1.0 / (deg_ref[...] + 1.0)
    sums = [
        pull_sum(ids, cols, tiles_ref, own_ref, sib_ref, b, i * ROWS_PER + b, n, steps - 1)
        for b in range(ROWS_PER)
    ]
    gathered = acc_ref[...] + jnp.concatenate(sums, axis=0)
    aggregate = (gathered * inverse).astype(BF16)
    agg_ref[...] = aggregate
    pre = mm(feat_ref[...], wself_ref[...]) + mm(aggregate, wneigh_ref[...])
    pre = pre + bias_ref[...].astype(F32)
    slope = 0.7978845608028654
    square = pre * pre
    bent = jnp.tanh(slope * (pre + 0.044715 * (square * pre)))
    half = 0.5 * (1.0 + bent)
    out_ref[...] = (pre * half).astype(BF16)
    deriv = half + (0.5 * pre) * (1.0 - bent * bent) * (slope + (3 * 0.044715 * slope) * square)
    grad_pre = (cot_ref[...].astype(F32) * deriv).astype(BF16)
    gp_ref[...] = grad_pre
    signal = (mm(grad_pre, wneigh_ref[...], 1, 1) * inverse).astype(BF16)
    sig_ref[...] = signal
    core, chip = ids[0], ids[2]
    for b in range(ROWS_PER):
        place(
            cols, lambda which, b=b: turned_ref[b, which], signal[b * BLK : (b + 1) * BLK],
            place_ref, i * ROWS_PER + b, core, chip, n,
        )

    @pl.when(i == pl.num_programs(0) - 1)
    def _():
        keep_ref[...] = place_ref[0].astype(BF16)
        send_ref[...] = place_ref[1].astype(BF16)


def middle(ids, cols, tiles, turned, own, sib, acc, deg, features, cot, w_self, w_neigh, bias, steps):
    g, n = tiles.shape[:2]
    rows, width = features.shape
    outw = w_self.shape[1]
    tall = ROWS_PER * BLK

    def whole(r, c):
        return pl.BlockSpec((r, c), lambda i, ids, cols: (0, 0))

    def part(c):
        return pl.BlockSpec((tall, c), lambda i, ids, cols: (i, 0))

    def pair(at):
        return pl.BlockSpec((ROWS_PER, 2, BLK, BLK), lambda i, ids, cols: (i, ids[at], 0, 0))

    def shape(c, t):
        return jax.ShapeDtypeStruct((rows, c), t)

    return pl.pallas_call(
        partial(middle_kernel, n=n, steps=steps),
        grid_spec=pltpu.PrefetchScalarGridSpec(
            num_scalar_prefetch=2,
            grid=(g // ROWS_PER,),
            in_specs=[
                pair(steps), whole(rows, width), whole(rows, width), part(width), part(width),
                part(width), part(outw), whole(width, outw), whole(width, outw), whole(1, outw),
                pair(2),
            ],
            out_specs=[
                part(outw), part(outw), part(width), part(width),
                whole(rows, width), whole(rows, width),
            ],
            scratch_shapes=[pltpu.VMEM((2, rows, width), F32)],
        ),
        out_shape=[
            shape(outw, BF16), shape(outw, BF16), shape(width, BF16), shape(width, BF16),
            shape(width, BF16), shape(width, BF16),
        ],
        compiler_params=params(),
        cost_estimate=cost(8 * rows * BLK * width + 6 * rows * width * outw, 30 * rows * width, rows * outw),
        name="middle",
    )(ids, cols, tiles, own, sib, acc, deg, features, cot, w_self, w_neigh, bias, turned)


def push_kernel(ids, cols, sig_ref, turned_ref, keep_ref, send_ref, place_ref, *, n, steps):
    p = pl.program_id(0)
    chip = ids[1 + lax.rem(p + 2, steps)]
    place_ref[...] = jnp.zeros_like(place_ref)
    for g in range(turned_ref.shape[0]):
        place(
            cols, lambda which, g=g: turned_ref[g, which], sig_ref[g * BLK : (g + 1) * BLK, :],
            place_ref, g, ids[0], chip, n,
        )
    keep_ref[0] = place_ref[0].astype(BF16)
    send_ref[0] = place_ref[1].astype(BF16)


def push(ids, cols, signal, turned, steps):
    g, n = turned.shape[:2]
    rows, width = signal.shape
    out = pl.BlockSpec((1, rows, width), lambda p, ids, cols: (p, 0, 0))
    return pl.pallas_call(
        partial(push_kernel, n=n, steps=steps),
        grid_spec=pltpu.PrefetchScalarGridSpec(
            num_scalar_prefetch=2,
            grid=(steps - 1,),
            in_specs=[
                pl.BlockSpec((rows, width), lambda p, ids, cols: (0, 0)),
                pl.BlockSpec(
                    (g, 2, BLK, BLK),
                    lambda p, ids, cols: (0, ids[1 + lax.rem(p + 2, steps)], 0, 0),
                ),
            ],
            out_specs=[out, out],
            scratch_shapes=[pltpu.VMEM((2, rows, width), F32)],
        ),
        out_shape=[jax.ShapeDtypeStruct((steps - 1, rows, width), BF16)] * 2,
        compiler_params=params(),
        cost_estimate=cost(4 * (steps - 1) * rows * BLK * width, 8 * (steps - 1) * rows * width),
        name="push",
    )(ids, cols, signal, turned)


def split(x):
    high = x.astype(BF16)
    return high, (x - high.astype(F32)).astype(BF16)


def message_kernel(asked, row, valid, off_ref, sig_ref, feat_ref, agg_ref, gp_ref, msg_ref, *, wide):
    here = lax.axis_index("wide")
    tall = 4 * BLK
    dself = dneigh = dbias = None
    for i in range(feat_ref.shape[0] // tall):
        rows = pl.ds(i * tall, tall)
        gp = gp_ref[rows, :]
        a = mm(feat_ref[rows, :], gp, 0, 0)
        b = mm(agg_ref[rows, :], gp, 0, 0)
        c = jnp.sum(gp.astype(F32), axis=0, keepdims=True)
        dself, dneigh, dbias = (a, b, c) if i == 0 else (dself + a, dneigh + b, dbias + c)
    parts = []
    for d in (dself, dneigh):
        high, low = split(d)
        parts += [high[:, :BLK], high[:, BLK:], low[:, :BLK], low[:, BLK:]]
    grads = jnp.concatenate(parts, axis=0)
    bias_high, bias_low = split(jnp.broadcast_to(dbias, (16, 2 * BLK)))
    line = lax.broadcasted_iota(jnp.int32, (16, BLK), 0)
    for k in range(wide):
        peer = target(here, k, wide)
        mask = (off_ref[0, peer] * valid[peer]).astype(F32).astype(BF16)
        at = pl.ds(pl.multiple_of(row[peer] * BLK, BLK), BLK)
        msg_ref[k, pl.ds(0, BLK), :] = mm(mask, sig_ref[at, :], 0, 0).astype(BF16)
        index = jnp.full((16, BLK), asked[peer], jnp.int32).astype(F32)
        extra = jnp.where(line == 0, index, 0.0)
        for r, v in enumerate(
            (bias_high[:, :BLK], bias_high[:, BLK:], bias_low[:, :BLK], bias_low[:, BLK:])
        ):
            extra = jnp.where(line == r + 1, v.astype(F32), extra)
        msg_ref[k, pl.ds(BLK, 16), :] = extra.astype(BF16)
        msg_ref[k, pl.ds(BLK + 16, 8 * BLK), :] = grads


def messages(asked, row, valid, off_tiles, signal, features, aggregate, grad_pre):
    wide = off_tiles.shape[1]
    tall = 9 * BLK + 16
    rows, width = features.shape

    def whole(x):
        return pl.BlockSpec(x.shape, lambda i, *s: (0,) * x.ndim)

    ins = (off_tiles, signal, features, aggregate, grad_pre)
    return pl.pallas_call(
        partial(message_kernel, wide=wide),
        grid_spec=pltpu.PrefetchScalarGridSpec(
            num_scalar_prefetch=3,
            grid=(1,),
            in_specs=[whole(x) for x in ins],
            out_specs=pl.BlockSpec((wide, tall, width), lambda i, *s: (0, 0, 0)),
        ),
        out_shape=jax.ShapeDtypeStruct((wide, tall, width), BF16),
        compiler_params=params(),
        cost_estimate=cost(8 * rows * width * width, 16 * rows * width),
        name="messages",
    )(asked, row, valid, *ins)


def base_kernel(places, gp_ref, wself_ref, keep_ref, come_ref, pushed_ref, out_ref):
    tall = 4 * BLK
    for i in range(out_ref.shape[0] // tall):
        rows = pl.ds(i * tall, tall)
        both = keep_ref[rows, :].astype(F32) + come_ref[rows, :].astype(F32)
        out_ref[rows, :] = mm(gp_ref[rows, :], wself_ref[...], 1, 1) + both
    for k in range(pushed_ref.shape[0]):
        at = pl.ds(pl.multiple_of(places[k] * BLK, BLK), BLK)
        out_ref[at, :] += pushed_ref[k].astype(F32)


def base(places, grad_pre, w_self, keep, come, pushed):
    rows, width = keep.shape

    def whole(x):
        return pl.BlockSpec(x.shape, lambda i, *s: (0,) * x.ndim)

    ins = (grad_pre, w_self, keep, come, pushed)
    return pl.pallas_call(
        base_kernel,
        grid_spec=pltpu.PrefetchScalarGridSpec(
            num_scalar_prefetch=1,
            grid=(1,),
            in_specs=[whole(x) for x in ins],
            out_specs=pl.BlockSpec((rows, width), lambda i, *s: (0, 0)),
        ),
        out_shape=jax.ShapeDtypeStruct((rows, width), F32),
        compiler_params=params(),
        cost_estimate=cost(4 * rows * width * width, 12 * rows * width),
        name="base",
    )(places, *ins)


def power(size):
    return size & (size - 1) == 0


def target(i, k, size):
    return i ^ k if power(size) else lax.rem(i + k, size)


def source(i, k, size):
    return i ^ k if power(size) else lax.rem(i + size - k, size)


def to_peer(x, axis, k):
    size = lax.axis_size(axis)
    return lax.ppermute(x, axis, [(i, i ^ k if power(size) else (i + k) % size) for i in range(size)])


def tree_sum(parts):
    while len(parts) > 1:
        pairs = [a + b for a, b in zip(parts[::2], parts[1::2])]
        parts = pairs + parts[len(pairs) * 2 :]
    return parts[0]


def shards(
    features,
    band_tiles,
    band_cols,
    off_tiles,
    req_block,
    req_row,
    req_valid,
    weight_self,
    weight_neigh,
    bias_term,
    cotangent,
):
    row_count, width = features.shape
    n = lax.axis_size("narrow")
    wide = lax.axis_size("wide")
    steps = n // 2
    fold = [0] + list(range(1, steps, 2)) + list(range(2, steps, 2))[::-1]
    after = {a: b for a, b in zip(fold, fold[1:] + fold[:1])}

    def onward(x):
        return lax.ppermute(x, "narrow", [(i, after[i // 2] * 2 + i % 2) for i in range(n)])

    def swap(x):
        return to_peer(x, "narrow", 1)

    me = lax.axis_index("narrow")
    here = lax.axis_index("wide")
    chips = jnp.array(
        [[fold[(fold.index(z) - s) % steps] for s in range(steps)] for z in range(steps)], jnp.int32
    )[me // 2]
    ids = jnp.concatenate([(me % 2)[None].astype(jnp.int32), chips])
    cols = band_cols.reshape(-1)
    asked, row, valid = req_block[0], req_row[0], req_valid[0]
    sources = jnp.stack([source(here, k, wide) for k in range(wide)])
    asked_by = jnp.concatenate([asked, asked[sources]])

    own, sib = features, swap(features)
    by_peer = [features] + [to_peer(features, "wide", k) for k in range(1, wide)]
    tiles, turned, degree = prep(band_tiles)
    acc = None
    for s in range(steps - 1):
        following = onward(own)
        acc = pull(ids, cols, tiles, own, sib, acc, s)
        own = following
        sib = swap(own)
    acc, degree = off_band(asked_by, row, valid, off_tiles, by_peer, acc, degree)
    layer_out, grad_pre, aggregate, signal, keep, send = middle(
        ids, cols, tiles, turned, own, sib, acc, degree, features, cotangent,
        weight_self, weight_neigh, bias_term.reshape(1, -1), steps,
    )

    going = (keep.astype(F32) + swap(send).astype(F32)).astype(BF16)
    keeps, sends = push(ids, cols, signal, turned, steps)
    come = swap(sends)
    for s in range(steps - 2):
        got = onward(going)
        going = (got.astype(F32) + (keeps[s].astype(F32) + come[s].astype(F32))).astype(BF16)
    got = onward(going)

    msgs = messages(asked, row, valid, off_tiles, signal, features, aggregate, grad_pre)
    arrived = [msgs[0]] + [to_peer(msgs[k], "wide", k) for k in range(1, wide)]
    places = jnp.stack([a[BLK, 0] for a in arrived]).astype(jnp.int32)
    pushed = jnp.stack([a[:BLK] for a in arrived])
    rest = base(places, grad_pre, weight_self, keeps[-1], come[-1], pushed)
    grad_features = rest + got.astype(F32)

    def grads_of(a):
        g = a[BLK + 16 :].reshape(2, 2, 2, BLK, BLK).astype(F32)
        g = (g[:, 0] + g[:, 1]).transpose(0, 2, 1, 3).reshape(2, BLK, 2 * BLK)
        e = a[BLK + 1 : BLK + 5].astype(F32)
        e = (e[:2] + e[2:]).reshape(1, 1, 2 * BLK)
        e = jnp.concatenate([e, jnp.zeros((1, 1, 2 * BLK), F32)], axis=0)
        e = jnp.concatenate([e, jnp.zeros((2, 7, 2 * BLK), F32)], axis=1)
        return jnp.concatenate([g, e], axis=1)

    sums = tree_sum([grads_of(a) for a in arrived])
    core = me % 2
    mine = lax.dynamic_index_in_dim(sums, core, 0, keepdims=False)
    other = lax.dynamic_index_in_dim(sums, 1 - core, 0, keepdims=False)
    total = mine + swap(other)
    if power(steps):
        k = 1
        while k < steps:
            total = total + to_peer(total, "narrow", 2 * k)
            k *= 2
    else:
        total = lax.psum(total, "narrow", axis_index_groups=[list(range(c, n, 2)) for c in (0, 1)])
    total = total * ((wide * n * row_count) ** (-0.5))
    paired = swap(total)
    first = jnp.where(core == 0, total, paired)
    second = jnp.where(core == 0, paired, total)
    return layer_out, grad_features, first[:BLK], second[:BLK], first[BLK]


def solution(mesh):
    both = ("wide", "narrow")
    placed = (
        P(both, None),
        P(both, None, None, None),
        P(both, None),
        P(both, None, None, None),
        P(both, None),
        P(both, None),
        P(both, None),
        P(),
        P(),
        P(),
        P(both, None),
    )
    return jax.shard_map(
        shards,
        mesh=mesh,
        in_specs=placed,
        out_specs=(P(both, None), P(both, None), P(), P(), P()),
        check_vma=False,
    )
```

```python
from functools import partial

import jax
import jax.numpy as jnp
from jax import lax
from jax.experimental import pallas as pl
from jax.experimental.pallas import tpu as pltpu
from jax.sharding import PartitionSpec as P

F32 = jnp.float32
BF16 = jnp.bfloat16
BLK = 128
ROWS_PER = 4
CHUNKS = 2
VMEM = 20 * 1024 * 1024


def mm(a, b, lhs=1, rhs=0):
    return lax.dot_general(a, b, (((lhs,), (rhs,)), ((), ())), preferred_element_type=F32)


def params():
    return pltpu.CompilerParams(vmem_limit_bytes=VMEM)


def cost(flops, nbytes, trans=0):
    return pl.CostEstimate(flops=flops, bytes_accessed=nbytes, transcendentals=trans)


def prep_kernel(t_ref, plain_ref, deg_ref):
    total = jnp.zeros((BLK, BLK), F32)
    for k in range(t_ref.shape[1]):
        t = t_ref[0, k].astype(F32)
        total = total + t
        plain_ref[0, k] = t.astype(BF16)
    deg_ref[...] = jnp.broadcast_to(jnp.sum(total, axis=1, keepdims=True), (BLK, BLK))


def prep(tiles):
    g, n = tiles.shape[:2]
    tile_spec = pl.BlockSpec((1, n, BLK, BLK), lambda i: (i, 0, 0, 0))
    return pl.pallas_call(
        prep_kernel,
        grid=(g,),
        in_specs=[tile_spec],
        out_specs=[tile_spec, pl.BlockSpec((BLK, BLK), lambda i: (i, 0))],
        out_shape=[
            jax.ShapeDtypeStruct(tiles.shape, BF16),
            jax.ShapeDtypeStruct((g * BLK, BLK), F32),
        ],
        compiler_params=params(),
        cost_estimate=cost(tiles.size, tiles.size * 8),
        name="prep",
    )(tiles)


def block(ref, index):
    return ref[pl.ds(pl.multiple_of(index * BLK, BLK), BLK), :]


def pull_sum(ids, cols, tiles_ref, slabs_ref, b, g, n, step):
    core, chip = ids[0], ids[1 + step]
    own = block(slabs_ref.at[0], cols[g * n + chip * 2 + core])
    sib = block(slabs_ref.at[1], cols[g * n + chip * 2 + 1 - core])
    return mm(tiles_ref[b, core], own) + mm(tiles_ref[b, 1 - core], sib)


def lay_out(parts, slabs_ref):
    tall = parts[0].shape[0]
    for j, part in enumerate(parts):
        half, at = divmod(j, len(parts) // 2)
        slabs_ref[half, pl.ds(at * tall, tall), :] = part[...]


def pull_kernel(ids, cols, tiles_ref, *refs, n, step, first):
    if first:
        *parts, out_ref, slabs_ref = refs
    else:
        *parts, acc_ref, out_ref, slabs_ref = refs
    lay_out(parts, slabs_ref)
    for g in range(tiles_ref.shape[0]):
        rows = pl.ds(g * BLK, BLK)
        part = pull_sum(ids, cols, tiles_ref, slabs_ref, g, g, n, step)
        out_ref[rows, :] = part if first else acc_ref[rows, :] + part


def pull(ids, cols, tiles, own, sib, acc, step):
    g, n = tiles.shape[:2]
    width = own[0].shape[1]
    rows = g * BLK
    whole = pl.BlockSpec((rows, width), lambda i, ids, cols: (0, 0))
    chunk = pl.BlockSpec(own[0].shape, lambda i, ids, cols: (0, 0))
    pair = pl.BlockSpec((g, 2, BLK, BLK), lambda i, ids, cols: (0, ids[1 + step], 0, 0))
    more = () if acc is None else (acc,)
    return pl.pallas_call(
        partial(pull_kernel, n=n, step=step, first=acc is None),
        grid_spec=pltpu.PrefetchScalarGridSpec(
            num_scalar_prefetch=2,
            grid=(1,),
            in_specs=[pair] + [chunk] * (len(own) + len(sib)) + [whole] * len(more),
            out_specs=whole,
            scratch_shapes=[pltpu.VMEM((2, rows, width), BF16)],
        ),
        out_shape=jax.ShapeDtypeStruct((rows, width), F32),
        compiler_params=params(),
        cost_estimate=cost(4 * rows * BLK * width, 12 * rows * width),
        name=f"pull{step}",
    )(ids, cols, tiles, *own, *sib, *more)


def off_kernel(here_ref, asked, row, valid, off_ref, *refs, wide):
    fetched, (acc_in, deg_in, acc_ref, deg_ref) = refs[:wide], refs[wide:]
    acc_ref[...] = acc_in[...]
    deg_ref[...] = deg_in[...]
    here = here_ref[0]
    for k in range(wide):
        src = source(here, k, wide)
        mask = off_ref[0, src].astype(F32) * valid[src].astype(F32)
        at = pl.ds(pl.multiple_of(row[src] * BLK, BLK), BLK)
        acc_ref[at, :] += mm(mask.astype(BF16), fetched[k][...])
        deg_ref[at, :] += jnp.broadcast_to(jnp.sum(mask, axis=1, keepdims=True), (BLK, BLK))


def off_band(here, asked, row, valid, off_tiles, by_peer, acc, deg):
    wide = len(by_peer)
    rows, width = acc.shape

    def spec_of(k):
        return pl.BlockSpec(
            (BLK, width), lambda i, here, asked, row, valid: (asked[source(here[0], k, wide)], 0)
        )

    full = pl.BlockSpec((rows, width), lambda i, *s: (0, 0))
    offs = pl.BlockSpec(off_tiles.shape, lambda i, *s: (0, 0, 0, 0))
    return pl.pallas_call(
        partial(off_kernel, wide=wide),
        grid_spec=pltpu.PrefetchScalarGridSpec(
            num_scalar_prefetch=4,
            grid=(1,),
            in_specs=[offs] + [spec_of(k) for k in range(wide)] + [full, full],
            out_specs=[full, full],
        ),
        out_shape=[jax.ShapeDtypeStruct((rows, width), F32)] * 2,
        compiler_params=params(),
        cost_estimate=cost(2 * wide * BLK**3, 16 * rows * width),
        name="off_band",
    )(here, asked, row, valid, off_tiles, *by_peer, acc, deg)


def place(cols, tile, signal_rows, place_ref, g, core, chip, n):
    for j in range(2):
        which = core if j == 0 else 1 - core
        at = pl.ds(pl.multiple_of(cols[g * n + chip * 2 + which] * BLK, BLK), BLK)
        place_ref[j, at, :] += mm(tile(which), signal_rows, 0, 0)


def middle_kernel(
    ids, cols, tiles_ref, acc_ref, deg_ref, feat_ref, cot_ref,
    wself_ref, wneigh_ref, bias_ref, going_ref, *refs, n, steps,
):
    *parts, out_ref, gp_ref, agg_ref, sig_ref, keep_ref, send_ref, place_ref, slabs_ref = refs
    i = pl.program_id(0)

    @pl.when(i == 0)
    def _():
        place_ref[...] = jnp.zeros_like(place_ref)
        lay_out(parts, slabs_ref)

    inverse = 1.0 / (deg_ref[...] + 1.0)
    sums = [
        pull_sum(ids, cols, tiles_ref, slabs_ref, b, i * ROWS_PER + b, n, steps - 1)
        for b in range(ROWS_PER)
    ]
    gathered = acc_ref[...] + jnp.concatenate(sums, axis=0)
    aggregate = (gathered * inverse).astype(BF16)
    agg_ref[...] = aggregate
    pre = mm(feat_ref[...], wself_ref[...]) + mm(aggregate, wneigh_ref[...])
    pre = pre + bias_ref[...].astype(F32)
    slope = 0.7978845608028654
    square = pre * pre
    bent = jnp.tanh(slope * (pre + 0.044715 * (square * pre)))
    half = 0.5 * (1.0 + bent)
    out_ref[...] = (pre * half).astype(BF16)
    deriv = half + (0.5 * pre) * (1.0 - bent * bent) * (slope + (3 * 0.044715 * slope) * square)
    grad_pre = (cot_ref[...].astype(F32) * deriv).astype(BF16)
    gp_ref[...] = grad_pre
    signal = (mm(grad_pre, wneigh_ref[...], 1, 1) * inverse).astype(BF16)
    sig_ref[...] = signal
    core, chip = ids[0], ids[2]
    for b in range(ROWS_PER):
        place(
            cols, lambda which, b=b: going_ref[b, which], signal[b * BLK : (b + 1) * BLK],
            place_ref, i * ROWS_PER + b, core, chip, n,
        )

    @pl.when(i == pl.num_programs(0) - 1)
    def _():
        keep_ref[...] = place_ref[0].astype(BF16)
        send_ref[...] = place_ref[1].astype(BF16)


def middle(ids, cols, tiles, own, sib, acc, deg, features, cot, w_self, w_neigh, bias, steps):
    g, n = tiles.shape[:2]
    rows, width = features.shape
    outw = w_self.shape[1]
    tall = ROWS_PER * BLK

    def whole(r, c):
        return pl.BlockSpec((r, c), lambda i, ids, cols: (0, 0))

    def part(c):
        return pl.BlockSpec((tall, c), lambda i, ids, cols: (i, 0))

    def pair(at):
        return pl.BlockSpec((ROWS_PER, 2, BLK, BLK), lambda i, ids, cols: (i, ids[at], 0, 0))

    def shape(c, t):
        return jax.ShapeDtypeStruct((rows, c), t)

    return pl.pallas_call(
        partial(middle_kernel, n=n, steps=steps),
        grid_spec=pltpu.PrefetchScalarGridSpec(
            num_scalar_prefetch=2,
            grid=(g // ROWS_PER,),
            in_specs=[
                pair(steps), part(width), part(width), part(width), part(outw),
                whole(width, outw), whole(width, outw), whole(1, outw), pair(2),
            ]
            + [whole(*x.shape) for x in (*own, *sib)],
            out_specs=[
                part(outw), part(outw), part(width), part(width),
                whole(rows, width), whole(rows, width),
            ],
            scratch_shapes=[
                pltpu.VMEM((2, rows, width), F32),
                pltpu.VMEM((2, rows, width), BF16),
            ],
        ),
        out_shape=[
            shape(outw, BF16), shape(outw, BF16), shape(width, BF16), shape(width, BF16),
            shape(width, BF16), shape(width, BF16),
        ],
        compiler_params=params(),
        cost_estimate=cost(8 * rows * BLK * width + 6 * rows * width * outw, 30 * rows * width, rows * outw),
        name="middle",
    )(ids, cols, tiles, acc, deg, features, cot, w_self, w_neigh, bias, tiles, *own, *sib)


def push_kernel(ids, cols, sig_ref, tiles_ref, keep_ref, send_ref, place_ref, *, n, steps):
    p = pl.program_id(0)
    chip = ids[1 + lax.rem(p + 2, steps)]
    place_ref[...] = jnp.zeros_like(place_ref)
    for g in range(tiles_ref.shape[0]):
        place(
            cols, lambda which, g=g: tiles_ref[g, which], sig_ref[g * BLK : (g + 1) * BLK, :],
            place_ref, g, ids[0], chip, n,
        )
    keep_ref[0] = place_ref[0].astype(BF16)
    send_ref[0] = place_ref[1].astype(BF16)


def push(ids, cols, signal, tiles, steps):
    g, n = tiles.shape[:2]
    rows, width = signal.shape
    out = pl.BlockSpec((1, rows, width), lambda p, ids, cols: (p, 0, 0))
    return pl.pallas_call(
        partial(push_kernel, n=n, steps=steps),
        grid_spec=pltpu.PrefetchScalarGridSpec(
            num_scalar_prefetch=2,
            grid=(steps - 1,),
            in_specs=[
                pl.BlockSpec((rows, width), lambda p, ids, cols: (0, 0)),
                pl.BlockSpec(
                    (g, 2, BLK, BLK),
                    lambda p, ids, cols: (0, ids[1 + lax.rem(p + 2, steps)], 0, 0),
                ),
            ],
            out_specs=[out, out],
            scratch_shapes=[pltpu.VMEM((2, rows, width), F32)],
        ),
        out_shape=[jax.ShapeDtypeStruct((steps - 1, rows, width), BF16)] * 2,
        compiler_params=params(),
        cost_estimate=cost(4 * (steps - 1) * rows * BLK * width, 8 * (steps - 1) * rows * width),
        name="push",
    )(ids, cols, signal, tiles)


def half_rows(wide):
    step = 16 * wide
    return (BLK + 1 + step - 1) // step * step


def grads_kernel(
    ids, asked, row, valid, off_ref, sig_ref, feat_ref, agg_ref, gp_ref,
    mine_ref, other_ref, *pushed_refs, wide,
):
    here = lax.axis_index("wide")
    tall = 4 * BLK
    dself = dneigh = dbias = None
    for i in range(feat_ref.shape[0] // tall):
        rows = pl.ds(i * tall, tall)
        gp = gp_ref[rows, :]
        a = mm(feat_ref[rows, :], gp, 0, 0)
        b = mm(agg_ref[rows, :], gp, 0, 0)
        c = jnp.sum(gp.astype(F32), axis=0, keepdims=True)
        dself, dneigh, dbias = (a, b, c) if i == 0 else (dself + a, dneigh + b, dbias + c)
    first = ids[0] == 0
    mine_ref[pl.ds(0, BLK), :] = jnp.where(first, dself, dneigh)
    other_ref[pl.ds(0, BLK), :] = jnp.where(first, dneigh, dself)
    spare = mine_ref.shape[0] - BLK
    mine_ref[pl.ds(BLK, spare), :] = jnp.broadcast_to(dbias, (spare, dbias.shape[1]))
    other_ref[pl.ds(BLK, spare), :] = jnp.broadcast_to(dbias, (spare, dbias.shape[1]))
    for k in range(wide):
        peer = target(here, k, wide)
        mask = (off_ref[0, peer] * valid[peer]).astype(F32).astype(BF16)
        at = pl.ds(pl.multiple_of(row[peer] * BLK, BLK), BLK)
        ref = pushed_refs[k]
        ref[pl.ds(0, BLK), :] = mm(mask, sig_ref[at, :], 0, 0).astype(BF16)
        ref[pl.ds(BLK, 16), :] = jnp.full((16, BLK), asked[peer], jnp.int32).astype(F32).astype(BF16)


def grads(ids, asked, row, valid, off_tiles, signal, features, aggregate, grad_pre):
    wide = off_tiles.shape[1]
    rows, width = features.shape
    outw = grad_pre.shape[1]

    def whole(x):
        return pl.BlockSpec(x.shape, lambda i, *s: (0,) * len(x.shape))

    ins = (off_tiles, signal, features, aggregate, grad_pre)
    outs = [jax.ShapeDtypeStruct((half_rows(wide), outw), F32)] * 2
    outs += [jax.ShapeDtypeStruct((BLK + 16, width), BF16)] * wide
    return pl.pallas_call(
        partial(grads_kernel, wide=wide),
        grid_spec=pltpu.PrefetchScalarGridSpec(
            num_scalar_prefetch=4,
            grid=(1,),
            in_specs=[whole(x) for x in ins],
            out_specs=[whole(x) for x in outs],
        ),
        out_shape=outs,
        compiler_params=params(),
        cost_estimate=cost(8 * rows * width * width, 16 * rows * width),
        name="grads",
    )(ids, asked, row, valid, *ins)


def pack_kernel(mine_ref, come_ref, *refs, wide):
    pushed_refs, msg_refs = refs[:wide], refs[wide:]
    here = lax.axis_index("wide")
    piece = mine_ref.shape[0] // wide
    head = BLK + 16
    for k in range(wide):
        peer = target(here, k, wide)
        rows = pl.ds(pl.multiple_of(peer * piece, 16), piece)
        total = mine_ref[rows, :] + come_ref[rows, :]
        high = total.astype(BF16)
        low = (total - high.astype(F32)).astype(BF16)
        msg_refs[k][pl.ds(0, head), :] = pushed_refs[k][...]
        for j, x in enumerate((high[:, :BLK], high[:, BLK:], low[:, :BLK], low[:, BLK:])):
            msg_refs[k][pl.ds(head + j * piece, piece), :] = x


def pack(mine, come, pushed):
    wide = len(pushed)

    def whole(x):
        return pl.BlockSpec(x.shape, lambda i: (0,) * len(x.shape))

    ins = (mine, come, *pushed)
    tall = BLK + 16 + mine.shape[0] // wide * 4
    outs = [jax.ShapeDtypeStruct((tall, pushed[0].shape[1]), BF16)] * wide
    return pl.pallas_call(
        partial(pack_kernel, wide=wide),
        grid=(1,),
        in_specs=[whole(x) for x in ins],
        out_specs=[whole(x) for x in outs],
        out_shape=outs,
        compiler_params=params(),
        cost_estimate=cost(4 * mine.size, 20 * mine.size),
        name="pack",
    )(*ins)


def piece_sum_kernel(*refs):
    arrived, out_ref = refs[:-1], refs[-1]
    piece = out_ref.shape[0]
    head = BLK + 16
    for side in range(2):
        part = [
            a[pl.ds(head + side * piece, piece), :].astype(F32)
            + a[pl.ds(head + (side + 2) * piece, piece), :].astype(F32)
            for a in arrived
        ]
        out_ref[:, pl.ds(side * BLK, BLK)] = tree_sum(part)


def piece_sum(arrived):
    def whole(x):
        return pl.BlockSpec(x.shape, lambda i: (0,) * len(x.shape))

    piece = (arrived[0].shape[0] - BLK - 16) // 4
    out = jax.ShapeDtypeStruct((piece, 2 * BLK), F32)
    return pl.pallas_call(
        piece_sum_kernel,
        grid=(1,),
        in_specs=[whole(x) for x in arrived],
        out_specs=whole(out),
        out_shape=out,
        compiler_params=params(),
        cost_estimate=cost(arrived[0].size * len(arrived), 2 * arrived[0].size * len(arrived)),
        name="piece_sum",
    )(*arrived)


def half_kernel(*refs, factor):
    pieces, out_ref = refs[:-1], refs[-1]
    wide, piece = len(pieces), pieces[0].shape[0]
    here = lax.axis_index("wide")
    for k in range(wide):
        at = pl.ds(pl.multiple_of(source(here, k, wide) * piece, 16), piece)
        out_ref[at, :] = pieces[k][...] * factor


def half(pieces, factor):
    def whole(x):
        return pl.BlockSpec(x.shape, lambda i: (0, 0))

    out = jax.ShapeDtypeStruct((pieces[0].shape[0] * len(pieces), pieces[0].shape[1]), F32)
    return pl.pallas_call(
        partial(half_kernel, factor=factor),
        grid=(1,),
        in_specs=[whole(x) for x in pieces],
        out_specs=whole(out),
        out_shape=out,
        compiler_params=params(),
        cost_estimate=cost(out.size, 8 * out.size),
        name="half",
    )(*pieces)


def finish_kernel(ids, total_ref, paired_ref, self_ref, neigh_ref, bias_ref):
    first = ids[0] == 0
    total, paired = total_ref[pl.ds(0, BLK), :], paired_ref[pl.ds(0, BLK), :]
    self_ref[...] = jnp.where(first, total, paired)
    neigh_ref[...] = jnp.where(first, paired, total)
    at = pl.ds(BLK, 8)
    bias_ref[...] = jnp.where(first, total_ref[at, :], paired_ref[at, :])[:1]


def finish(ids, total, paired):
    def whole(x):
        return pl.BlockSpec(x.shape, lambda i, *s: (0, 0))

    outs = [jax.ShapeDtypeStruct((r, 2 * BLK), F32) for r in (BLK, BLK, 1)]
    return pl.pallas_call(
        finish_kernel,
        grid_spec=pltpu.PrefetchScalarGridSpec(
            num_scalar_prefetch=1,
            grid=(1,),
            in_specs=[whole(total), whole(paired)],
            out_specs=[whole(x) for x in outs],
        ),
        out_shape=outs,
        compiler_params=params(),
        cost_estimate=cost(4 * total.size, 16 * total.size),
        name="finish",
    )(ids, total, paired)


def base_kernel(gp_ref, wself_ref, keep_ref, come_ref, *refs):
    arrived, out_ref = refs[:-1], refs[-1]
    tall = 4 * BLK
    for i in range(out_ref.shape[0] // tall):
        rows = pl.ds(i * tall, tall)
        both = keep_ref[0, rows, :].astype(F32) + come_ref[0, rows, :].astype(F32)
        out_ref[rows, :] = mm(gp_ref[rows, :], wself_ref[...], 1, 1) + both
    line = lax.broadcasted_iota(jnp.int32, (16, BLK), 0)
    for a in arrived:
        index = jnp.max(jnp.where(line == 0, a[pl.ds(BLK, 16), :].astype(F32), 0.0))
        at = pl.ds(pl.multiple_of(index.astype(jnp.int32) * BLK, BLK), BLK)
        out_ref[at, :] += a[pl.ds(0, BLK), :].astype(F32)


def base(grad_pre, w_self, keeps, comes, arrived):
    last, rows, width = keeps.shape

    def whole(x):
        return pl.BlockSpec(x.shape, lambda i, *s: (0,) * x.ndim)

    slab = pl.BlockSpec((1, rows, width), lambda i: (last - 1, 0, 0))
    head = pl.BlockSpec((BLK + 16, width), lambda i: (0, 0))
    return pl.pallas_call(
        base_kernel,
        grid=(1,),
        in_specs=[whole(grad_pre), whole(w_self), slab, slab] + [head] * len(arrived),
        out_specs=pl.BlockSpec((rows, width), lambda i, *s: (0, 0)),
        out_shape=jax.ShapeDtypeStruct((rows, width), F32),
        compiler_params=params(),
        cost_estimate=cost(4 * rows * width * width, 12 * rows * width),
        name="base",
    )(grad_pre, w_self, keeps, comes, *arrived)


def joined_kernel(*refs):
    total = refs[0][...].astype(F32)
    for ref in refs[1:-1]:
        total = total + ref[...].astype(F32)
    refs[-1][...] = total.astype(BF16)


def joined(j, got, stacks, s):
    last, rows, width = stacks[0].shape
    tall = rows // CHUNKS
    part = pl.BlockSpec((None, tall, width), lambda i: (s, j, 0))
    whole = pl.BlockSpec((tall, width), lambda i: (0, 0))
    more = () if got is None else (got,)
    return pl.pallas_call(
        joined_kernel,
        grid=(1,),
        in_specs=[whole] * len(more) + [part] * len(stacks),
        out_specs=whole,
        out_shape=jax.ShapeDtypeStruct((tall, width), BF16),
        compiler_params=params(),
        cost_estimate=cost(3 * tall * width, 8 * tall * width),
        name=f"joined{s}_{j}",
    )(*more, *stacks)


def last_kernel(rest_ref, *refs):
    got, out_ref = refs[:-1], refs[-1]
    tall = got[0].shape[0]
    for j, ref in enumerate(got):
        rows = pl.ds(j * tall, tall)
        out_ref[rows, :] = rest_ref[rows, :] + ref[...].astype(F32)


def last(rest, got):
    def whole(x):
        return pl.BlockSpec(x.shape, lambda i: (0, 0))

    return pl.pallas_call(
        last_kernel,
        grid=(1,),
        in_specs=[whole(x) for x in (rest, *got)],
        out_specs=whole(rest),
        out_shape=jax.ShapeDtypeStruct(rest.shape, F32),
        compiler_params=params(),
        cost_estimate=cost(rest.size, 10 * rest.size),
        name="last",
    )(rest, *got)


def power(size):
    return size & (size - 1) == 0


def target(i, k, size):
    return i ^ k if power(size) else lax.rem(i + k, size)


def source(i, k, size):
    return i ^ k if power(size) else lax.rem(i + size - k, size)


def to_peer(x, axis, k):
    size = lax.axis_size(axis)
    return lax.ppermute(x, axis, [(i, i ^ k if power(size) else (i + k) % size) for i in range(size)])


def tree_sum(parts):
    while len(parts) > 1:
        pairs = [a + b for a, b in zip(parts[::2], parts[1::2])]
        parts = pairs + parts[len(pairs) * 2 :]
    return parts[0]


def shards(
    features,
    band_tiles,
    band_cols,
    off_tiles,
    req_block,
    req_row,
    req_valid,
    weight_self,
    weight_neigh,
    bias_term,
    cotangent,
):
    row_count, width = features.shape
    n = lax.axis_size("narrow")
    wide = lax.axis_size("wide")
    steps = n // 2
    fold = [0] + list(range(1, steps, 2)) + list(range(2, steps, 2))[::-1]
    after = {a: b for a, b in zip(fold, fold[1:] + fold[:1])}

    def onward(x):
        return lax.ppermute(x, "narrow", [(i, after[i // 2] * 2 + i % 2) for i in range(n)])

    def swap(x):
        return to_peer(x, "narrow", 1)

    me = lax.axis_index("narrow")
    here = lax.axis_index("wide")
    chips = jnp.array(
        [[fold[(fold.index(z) - s) % steps] for s in range(steps)] for z in range(steps)], jnp.int32
    )[me // 2]
    ids = jnp.concatenate([(me % 2)[None].astype(jnp.int32), chips])
    cols = band_cols.reshape(-1)
    asked, row, valid = req_block[0], req_row[0], req_valid[0]
    def tie(*xs):
        return lax.optimization_barrier(xs)

    def cut(x):
        tall = row_count // CHUNKS
        return [lax.slice_in_dim(x, j * tall, (j + 1) * tall) for j in range(CHUNKS)]

    slabs, pairs = [cut(features)], []
    by_peer = [features] + [to_peer(features, "wide", k) for k in range(1, wide)]
    tiles, degree = prep(band_tiles)
    acc = None
    for s in range(1, steps):
        following = [onward(x) for x in slabs[-1]]
        pairs.append([swap(x) for x in slabs[-1]])
        if s == 1:
            following[1], tiles, degree = tie(following[1], tiles, degree)
        else:
            acc = pull(ids, cols, tiles, slabs[s - 2], pairs[s - 2], acc, s - 2)
            following[1], acc = tie(following[1], acc)
        if s == steps - 1:
            following[0], *by_peer = tie(following[0], *by_peer)
            acc = pull(ids, cols, tiles, slabs[-1], pairs[-1], acc, s - 1)
            acc, degree = off_band(
                here[None], asked, row, valid, off_tiles, by_peer, acc, degree
            )
            following[0], acc, degree = tie(following[0], acc, degree)
        slabs.append(following)
    pairs.append([swap(x) for x in slabs[-1]])
    layer_out, grad_pre, aggregate, signal, keep, send = middle(
        ids, cols, tiles, slabs[-1], pairs[-1], acc, degree, features, cotangent,
        weight_self, weight_neigh, bias_term.reshape(1, -1), steps,
    )

    come = swap(send)
    mine, other, *pushed = grads(ids, asked, row, valid, off_tiles, signal, features, aggregate, grad_pre)
    come, mine, other, *pushed = tie(come, mine, other, *pushed)
    first = (keep[None], come[None])
    going = [joined(j, None, first, 0) for j in range(CHUNKS)]
    *going, signal = tie(*going, signal)
    got = [onward(x) for x in going]
    keeps, sends = push(ids, cols, signal, tiles, steps)
    comes = swap(sends)
    packed = pack(mine, swap(other), pushed)
    arrived = [packed[0]] + [to_peer(packed[k], "wide", k) for k in range(1, wide)]
    got[0], keeps, comes, *packed = tie(got[0], keeps, comes, *packed)
    rest = total = None
    for s in range(steps - 2):
        going = [joined(j, got[j], (keeps, comes), s) for j in range(CHUNKS)]
        got = [onward(x) for x in going]
        if s == 0:
            total = piece_sum(arrived)
            rest = base(grad_pre, weight_self, keeps, comes, arrived)
            got[0], total, rest = tie(got[0], total, rest)
    if power(steps):
        k = 1
        while k < steps:
            total = total + to_peer(total, "narrow", 2 * k)
            k *= 2
    else:
        total = lax.psum(total, "narrow", axis_index_groups=[list(range(c, n, 2)) for c in (0, 1)])
    pieces = [total] + [to_peer(total, "wide", k) for k in range(1, wide)]
    whole = half(pieces, (wide * n * row_count) ** (-0.5))
    grad_self, grad_neigh, grad_bias = finish(ids, whole, swap(whole))
    got[-1], grad_self, grad_neigh, grad_bias = tie(got[-1], grad_self, grad_neigh, grad_bias)
    grad_features = last(rest, got)
    return layer_out, grad_features, grad_self, grad_neigh, grad_bias.reshape(-1)


def solution(mesh):
    both = ("wide", "narrow")
    placed = (
        P(both, None),
        P(both, None, None, None),
        P(both, None),
        P(both, None, None, None),
        P(both, None),
        P(both, None),
        P(both, None),
        P(),
        P(),
        P(),
        P(both, None),
    )
    return jax.shard_map(
        shards,
        mesh=mesh,
        in_specs=placed,
        out_specs=(P(both, None), P(both, None), P(), P(), P()),
        check_vma=False,
    )
```

```python
from functools import partial

import jax
import jax.numpy as jnp
from jax import lax
from jax.experimental import pallas as pl
from jax.experimental.pallas import tpu as pltpu
from jax.sharding import PartitionSpec as P

F32 = jnp.float32
BF16 = jnp.bfloat16
BLK = 128
ROWS_PER = 4
CHUNKS = 1
PARTS = 2
VMEM = 28 * 1024 * 1024


def mm(a, b, lhs=1, rhs=0):
    return lax.dot_general(a, b, (((lhs,), (rhs,)), ((), ())), preferred_element_type=F32)


def params():
    return pltpu.CompilerParams(vmem_limit_bytes=VMEM)


def cost(flops, nbytes, trans=0):
    return pl.CostEstimate(flops=flops, bytes_accessed=nbytes, transcendentals=trans)


def block(ref, index):
    return ref[pl.ds(pl.multiple_of(index * BLK, BLK), BLK), :]


def tile_reads(tiles_ref, buffer, sems, chip):
    count = buffer.shape[0] // ROWS_PER
    reads = []
    for q in range(count):
        rows = pl.ds(q * ROWS_PER, ROWS_PER)
        reads.append(
            pltpu.make_async_copy(
                tiles_ref.at[rows, pl.ds(chip * 2, 2)], buffer.at[rows], sems.at[q]
            )
        )
    for r in reads:
        r.start()
    return reads


def pair_sum(ids, cols, pair, slabs_ref, g, n, chip, base=0):
    core = ids[0]
    own = block(slabs_ref.at[0], cols[g * n + chip * 2 + core])
    sib = block(slabs_ref.at[1], cols[g * n + chip * 2 + 1 - core])
    mine, other = pair[g, base + core].astype(F32), pair[g, base + 1 - core].astype(F32)
    return mm(mine.astype(BF16), own) + mm(other.astype(BF16), sib), mine + other


def lay_out(parts, slabs_ref):
    tall = parts[0].shape[0]
    for j, part in enumerate(parts):
        half, at = divmod(j, len(parts) // 2)
        slabs_ref[half, pl.ds(at * tall, tall), :] = part[...]


def spec(x):
    return pl.BlockSpec(x.shape, lambda *i: (0,) * len(x.shape))


def in_hbm():
    return pl.BlockSpec(memory_space=pltpu.HBM)


def halve_kernel(t_ref, out_ref):
    out_ref[...] = t_ref[...].astype(F32).astype(BF16)


def halve(tiles):
    g, n = tiles.shape[:2]
    one = pl.BlockSpec((1, n, BLK, BLK), lambda i: (i, 0, 0, 0))
    return pl.pallas_call(
        halve_kernel,
        grid=(g,),
        in_specs=[one],
        out_specs=one,
        out_shape=jax.ShapeDtypeStruct(tiles.shape, BF16),
        compiler_params=params(),
        cost_estimate=cost(tiles.size, 6 * tiles.size),
        name="halve",
    )(tiles)


def pull_kernel(ids, cols, *refs, n, step, chunks, wide):
    refs = list(refs)
    if wide:
        row, valid = refs[:2]
        refs = refs[2:]
    tiles_ref, parts = refs[0], refs[1 : 1 + 2 * chunks]
    refs = refs[1 + 2 * chunks :]
    if step:
        acc_in, counts_in = refs[:2]
        refs = refs[2:]
    if wide:
        off_ref, fetched = refs[0], refs[1 : 1 + wide]
        refs = refs[1 + wide :]
        here = lax.axis_index("wide")
    acc_ref, counts_ref, slabs_ref, pair, sems = refs[:5]
    chip = ids[1 + step]
    reads = tile_reads(tiles_ref, pair, sems, chip)
    lay_out(parts, slabs_ref)
    for q, r in enumerate(reads):
        r.wait()
        for g in range(q * ROWS_PER, (q + 1) * ROWS_PER):
            rows = pl.ds(g * BLK, BLK)
            part, count = pair_sum(ids, cols, pair, slabs_ref, g, n, chip)
            acc_ref[rows, :] = acc_in[rows, :] + part if step else part
            counts_ref[rows, :] = counts_in[rows, :] + count if step else count
    if wide:
        for k in range(wide):
            src = target(here, k, wide)
            mask = (off_ref[0, src] * valid[src]).astype(F32)
            at = pl.ds(pl.multiple_of(row[src] * BLK, BLK), BLK)
            acc_ref[at, :] += mm(mask.astype(BF16), fetched[k][...])
            counts_ref[at, :] += mask


def pull(ids, cols, tiles, own, sib, sums, step, off=()):
    g, n = tiles.shape[:2]
    width = own[0].shape[1]
    rows = g * BLK
    wide = 0
    scalars, ins = [], [*own, *sib, *sums]
    specs = [in_hbm()] + [spec(x) for x in ins]
    if off:
        *scalars, off_tiles, fetched = off
        wide = len(fetched)
        ins += [off_tiles, *fetched]
        specs += [spec(x) for x in (off_tiles, *fetched)]
    out = jax.ShapeDtypeStruct((rows, width), F32)
    return pl.pallas_call(
        partial(pull_kernel, n=n, step=step, chunks=len(own), wide=wide),
        grid_spec=pltpu.PrefetchScalarGridSpec(
            num_scalar_prefetch=2 + len(scalars),
            grid=(1,),
            in_specs=specs,
            out_specs=[spec(out)] * 2,
            scratch_shapes=[
                pltpu.VMEM((2, rows, width), BF16),
                pltpu.VMEM((g, 2, BLK, BLK), jnp.int32),
                pltpu.SemaphoreType.DMA((g // ROWS_PER,)),
            ],
        ),
        out_shape=[out] * 2,
        compiler_params=params(),
        cost_estimate=cost(4 * rows * BLK * width, 12 * rows * width),
        name=f"pull{step}",
    )(ids, cols, *scalars, tiles, *ins)


def serve_kernel(*refs, wide):
    asked, feat_ref, outs = refs[:wide], refs[wide], refs[wide + 1 :]
    here = lax.axis_index("wide")
    for k in range(wide):
        outs[k][...] = block(feat_ref, asked[k][here])


def serve(asked, features):
    wide = len(asked)
    out = jax.ShapeDtypeStruct((BLK, features.shape[1]), features.dtype)
    return pl.pallas_call(
        partial(serve_kernel, wide=wide),
        grid_spec=pltpu.PrefetchScalarGridSpec(
            num_scalar_prefetch=wide,
            grid=(1,),
            in_specs=[spec(features)],
            out_specs=[spec(out)] * wide,
        ),
        out_shape=[out] * wide,
        compiler_params=params(),
        cost_estimate=cost(0, 4 * features.size),
        name="serve",
    )(*asked, features)


def place(cols, tiles_ref, signal_rows, place_ref, g, core, chip, n):
    for j in range(2):
        which = core if j == 0 else 1 - core
        at = pl.ds(pl.multiple_of(cols[g * n + chip * 2 + which] * BLK, BLK), BLK)
        place_ref[j, at, :] += mm(tiles_ref[g, chip * 2 + which], signal_rows, 0, 0)


def middle_kernel(
    ids, cols, tiles_ref, cot_ref, acc_ref, counts_ref, feat_ref, wself_ref, wneigh_ref, bias_ref,
    *refs, n, steps, chunks,
):
    parts, refs = refs[: 2 * chunks], refs[2 * chunks :]
    out_hbm, gp_ref, agg_ref, sig_ref, keep_ref, send_ref = refs[:6]
    place_ref, slabs_ref, out, out_sems = refs[6:]
    core, last, first = ids[0], ids[steps], ids[2]
    tall = ROWS_PER * BLK
    count = feat_ref.shape[0] // tall

    def rows_of(q):
        return pl.ds(q * tall, tall)

    writes = [
        pltpu.make_async_copy(out.at[rows_of(q)], out_hbm.at[rows_of(q)], out_sems.at[q])
        for q in range(count)
    ]
    place_ref[...] = jnp.zeros_like(place_ref)
    lay_out(parts, slabs_ref)
    ones = jnp.ones((BLK, BLK), BF16)
    slope = 0.7978845608028654
    for q in range(count):
        rows = rows_of(q)
        both = [
            pair_sum(ids, cols, tiles_ref, slabs_ref, g, n, last, last * 2)
            for g in range(q * ROWS_PER, (q + 1) * ROWS_PER)
        ]
        gathered = acc_ref[rows, :] + jnp.concatenate([b[0] for b in both], axis=0)
        counts = counts_ref[rows, :] + jnp.concatenate([b[1] for b in both], axis=0)
        inverse = 1.0 / (mm(counts.astype(BF16), ones) + 1.0)
        aggregate = (gathered * inverse).astype(BF16)
        agg_ref[rows, :] = aggregate
        pre = mm(feat_ref[rows, :], wself_ref[...]) + mm(aggregate, wneigh_ref[...])
        pre = pre + bias_ref[...].astype(F32)
        square = pre * pre
        bent = jnp.tanh(slope * (pre + 0.044715 * (square * pre)))
        half = 0.5 * (1.0 + bent)
        out[rows, :] = (pre * half).astype(BF16)
        writes[q].start()
        deriv = half + (0.5 * pre) * (1.0 - bent * bent) * (
            slope + (3 * 0.044715 * slope) * square
        )
        grad_pre = (cot_ref[rows, :].astype(F32) * deriv).astype(BF16)
        gp_ref[rows, :] = grad_pre
        signal = (mm(grad_pre, wneigh_ref[...], 1, 1) * inverse).astype(BF16)
        sig_ref[rows, :] = signal
        for b in range(ROWS_PER):
            rows_b = signal[b * BLK : (b + 1) * BLK]
            place(cols, tiles_ref, rows_b, place_ref, q * ROWS_PER + b, core, first, n)
    keep_ref[...] = place_ref[0].astype(BF16)
    send_ref[...] = place_ref[1].astype(BF16)
    for w in writes:
        w.wait()


def middle(ids, cols, tiles, cot, sums, features, w_self, w_neigh, bias, own, sib, steps):
    g, n = tiles.shape[:2]
    rows, width = features.shape
    outw = w_self.shape[1]
    count = g // ROWS_PER

    def shape(c):
        return jax.ShapeDtypeStruct((rows, c), BF16)

    ins = (*sums, features, w_self, w_neigh, bias, *own, *sib)
    outs = [shape(outw), shape(outw), shape(width), shape(width), shape(width), shape(width)]
    return pl.pallas_call(
        partial(middle_kernel, n=n, steps=steps, chunks=len(own)),
        grid_spec=pltpu.PrefetchScalarGridSpec(
            num_scalar_prefetch=2,
            grid=(1,),
            in_specs=[spec(x) for x in (tiles, cot, *ins)],
            out_specs=[in_hbm()] + [spec(x) for x in outs[1:]],
            scratch_shapes=[
                pltpu.VMEM((2, rows, width), F32),
                pltpu.VMEM((2, rows, width), BF16),
                pltpu.VMEM((rows, outw), BF16),
                pltpu.SemaphoreType.DMA((count,)),
            ],
        ),
        out_shape=outs,
        compiler_params=params(),
        cost_estimate=cost(
            8 * rows * BLK * width + 6 * rows * width * outw, 30 * rows * width, rows * outw
        ),
        name="middle",
    )(ids, cols, tiles, cot, *ins)


def push_kernel(ids, cols, tiles_ref, sig_ref, keep_ref, *refs, n, which):
    *send_refs, place_ref = refs
    parts = len(send_refs) // len(which)
    tall = send_refs[0].shape[0]
    for p, s in enumerate(which):
        place_ref[...] = jnp.zeros_like(place_ref)
        for g in range(tiles_ref.shape[0]):
            rows = sig_ref[g * BLK : (g + 1) * BLK, :]
            place(cols, tiles_ref, rows, place_ref, g, ids[0], ids[1 + s], n)
        keep_ref[p] = place_ref[0].astype(BF16)
        for j in range(parts):
            send_refs[p * parts + j][...] = place_ref[1, pl.ds(j * tall, tall), :].astype(BF16)


def push(ids, cols, signal, tiles, which):
    g, n = tiles.shape[:2]
    rows, width = signal.shape
    count = len(which)
    outs = [jax.ShapeDtypeStruct((count, rows, width), BF16)]
    outs += [jax.ShapeDtypeStruct((rows // PARTS, width), BF16)] * (count * PARTS)
    keeps, *sends = pl.pallas_call(
        partial(push_kernel, n=n, which=which),
        grid_spec=pltpu.PrefetchScalarGridSpec(
            num_scalar_prefetch=2,
            grid=(1,),
            in_specs=[spec(tiles), spec(signal)],
            out_specs=[spec(x) for x in outs],
            scratch_shapes=[pltpu.VMEM((2, rows, width), F32)],
        ),
        out_shape=outs,
        compiler_params=params(),
        cost_estimate=cost(4 * count * rows * BLK * width, 8 * count * rows * width),
        name="push",
    )(ids, cols, tiles, signal)
    return keeps, sends


def half_rows(wide):
    step = 16 * wide
    return (BLK + 1 + step - 1) // step * step


def grads_kernel(
    ids, asked, row, valid, off_ref, sig_ref, feat_ref, agg_ref, gp_ref,
    mine_ref, other_ref, *pushed_refs, wide,
):
    here = lax.axis_index("wide")
    tall = 4 * BLK
    dself = dneigh = dbias = None
    for i in range(feat_ref.shape[0] // tall):
        rows = pl.ds(i * tall, tall)
        gp = gp_ref[rows, :]
        a = mm(feat_ref[rows, :], gp, 0, 0)
        b = mm(agg_ref[rows, :], gp, 0, 0)
        c = jnp.sum(gp.astype(F32), axis=0, keepdims=True)
        dself, dneigh, dbias = (a, b, c) if i == 0 else (dself + a, dneigh + b, dbias + c)
    first = ids[0] == 0
    mine_ref[pl.ds(0, BLK), :] = jnp.where(first, dself, dneigh)
    other_ref[pl.ds(0, BLK), :] = jnp.where(first, dneigh, dself)
    spare = mine_ref.shape[0] - BLK
    mine_ref[pl.ds(BLK, spare), :] = jnp.broadcast_to(dbias, (spare, dbias.shape[1]))
    other_ref[pl.ds(BLK, spare), :] = jnp.broadcast_to(dbias, (spare, dbias.shape[1]))
    for k in range(wide):
        peer = target(here, k, wide)
        mask = (off_ref[0, peer] * valid[peer]).astype(F32).astype(BF16)
        at = pl.ds(pl.multiple_of(row[peer] * BLK, BLK), BLK)
        ref = pushed_refs[k]
        ref[pl.ds(0, BLK), :] = mm(mask, sig_ref[at, :], 0, 0).astype(BF16)
        ref[pl.ds(BLK, 16), :] = jnp.full((16, BLK), asked[peer], jnp.int32).astype(F32).astype(BF16)


def grads(ids, asked, row, valid, off_tiles, signal, features, aggregate, grad_pre):
    wide = off_tiles.shape[1]
    rows, width = features.shape
    outw = grad_pre.shape[1]

    def whole(x):
        return pl.BlockSpec(x.shape, lambda i, *s: (0,) * len(x.shape))

    ins = (off_tiles, signal, features, aggregate, grad_pre)
    outs = [jax.ShapeDtypeStruct((half_rows(wide), outw), F32)] * 2
    outs += [jax.ShapeDtypeStruct((BLK + 16, width), BF16)] * wide
    return pl.pallas_call(
        partial(grads_kernel, wide=wide),
        grid_spec=pltpu.PrefetchScalarGridSpec(
            num_scalar_prefetch=4,
            grid=(1,),
            in_specs=[whole(x) for x in ins],
            out_specs=[whole(x) for x in outs],
        ),
        out_shape=outs,
        compiler_params=params(),
        cost_estimate=cost(8 * rows * width * width, 16 * rows * width),
        name="grads",
    )(ids, asked, row, valid, *ins)


def pack_kernel(mine_ref, come_ref, *refs, wide):
    pushed_refs, msg_refs = refs[:wide], refs[wide:]
    here = lax.axis_index("wide")
    piece = mine_ref.shape[0] // wide
    head = BLK + 16
    for k in range(wide):
        peer = target(here, k, wide)
        rows = pl.ds(pl.multiple_of(peer * piece, 16), piece)
        total = mine_ref[rows, :] + come_ref[rows, :]
        high = total.astype(BF16)
        low = (total - high.astype(F32)).astype(BF16)
        msg_refs[k][pl.ds(0, head), :] = pushed_refs[k][...]
        for j, x in enumerate((high[:, :BLK], high[:, BLK:], low[:, :BLK], low[:, BLK:])):
            msg_refs[k][pl.ds(head + j * piece, piece), :] = x


def pack(mine, come, pushed):
    wide = len(pushed)

    def whole(x):
        return pl.BlockSpec(x.shape, lambda i: (0,) * len(x.shape))

    ins = (mine, come, *pushed)
    tall = BLK + 16 + mine.shape[0] // wide * 4
    outs = [jax.ShapeDtypeStruct((tall, pushed[0].shape[1]), BF16)] * wide
    return pl.pallas_call(
        partial(pack_kernel, wide=wide),
        grid=(1,),
        in_specs=[whole(x) for x in ins],
        out_specs=[whole(x) for x in outs],
        out_shape=outs,
        compiler_params=params(),
        cost_estimate=cost(4 * mine.size, 20 * mine.size),
        name="pack",
    )(*ins)


def piece_sum_kernel(*refs):
    arrived, out_ref = refs[:-1], refs[-1]
    piece = out_ref.shape[0]
    head = BLK + 16
    for side in range(2):
        part = [
            a[pl.ds(head + side * piece, piece), :].astype(F32)
            + a[pl.ds(head + (side + 2) * piece, piece), :].astype(F32)
            for a in arrived
        ]
        out_ref[:, pl.ds(side * BLK, BLK)] = tree_sum(part)


def piece_sum(arrived):
    def whole(x):
        return pl.BlockSpec(x.shape, lambda i: (0,) * len(x.shape))

    piece = (arrived[0].shape[0] - BLK - 16) // 4
    out = jax.ShapeDtypeStruct((piece, 2 * BLK), F32)
    return pl.pallas_call(
        piece_sum_kernel,
        grid=(1,),
        in_specs=[whole(x) for x in arrived],
        out_specs=whole(out),
        out_shape=out,
        compiler_params=params(),
        cost_estimate=cost(arrived[0].size * len(arrived), 2 * arrived[0].size * len(arrived)),
        name="piece_sum",
    )(*arrived)


def half_kernel(*refs, factor):
    pieces, out_ref = refs[:-1], refs[-1]
    wide, piece = len(pieces), pieces[0].shape[0]
    here = lax.axis_index("wide")
    for k in range(wide):
        at = pl.ds(pl.multiple_of(source(here, k, wide) * piece, 16), piece)
        out_ref[at, :] = pieces[k][...] * factor


def half(pieces, factor):
    def whole(x):
        return pl.BlockSpec(x.shape, lambda i: (0, 0))

    out = jax.ShapeDtypeStruct((pieces[0].shape[0] * len(pieces), pieces[0].shape[1]), F32)
    return pl.pallas_call(
        partial(half_kernel, factor=factor),
        grid=(1,),
        in_specs=[whole(x) for x in pieces],
        out_specs=whole(out),
        out_shape=out,
        compiler_params=params(),
        cost_estimate=cost(out.size, 8 * out.size),
        name="half",
    )(*pieces)


def finish_kernel(ids, total_ref, paired_ref, self_ref, neigh_ref, bias_ref):
    first = ids[0] == 0
    total, paired = total_ref[pl.ds(0, BLK), :], paired_ref[pl.ds(0, BLK), :]
    self_ref[...] = jnp.where(first, total, paired)
    neigh_ref[...] = jnp.where(first, paired, total)
    at = pl.ds(BLK, 8)
    bias_ref[...] = jnp.where(first, total_ref[at, :], paired_ref[at, :])[:1]


def finish(ids, total, paired):
    def whole(x):
        return pl.BlockSpec(x.shape, lambda i, *s: (0, 0))

    outs = [jax.ShapeDtypeStruct((r, 2 * BLK), F32) for r in (BLK, BLK, 1)]
    return pl.pallas_call(
        finish_kernel,
        grid_spec=pltpu.PrefetchScalarGridSpec(
            num_scalar_prefetch=1,
            grid=(1,),
            in_specs=[whole(total), whole(paired)],
            out_specs=[whole(x) for x in outs],
        ),
        out_shape=outs,
        compiler_params=params(),
        cost_estimate=cost(4 * total.size, 16 * total.size),
        name="finish",
    )(ids, total, paired)


def base_kernel(gp_ref, wself_ref, keep_ref, *refs, parts):
    come, arrived, out_ref = refs[:parts], refs[parts:-1], refs[-1]
    tall = 4 * BLK
    for i in range(out_ref.shape[0] // tall):
        rows = pl.ds(i * tall, tall)
        out_ref[rows, :] = mm(gp_ref[rows, :], wself_ref[...], 1, 1) + keep_ref[rows, :].astype(F32)
    tall = come[0].shape[0]
    for j, part in enumerate(come):
        out_ref[pl.ds(j * tall, tall), :] += part[...].astype(F32)
    line = lax.broadcasted_iota(jnp.int32, (16, BLK), 0)
    for a in arrived:
        index = jnp.max(jnp.where(line == 0, a[pl.ds(BLK, 16), :].astype(F32), 0.0))
        at = pl.ds(pl.multiple_of(index.astype(jnp.int32) * BLK, BLK), BLK)
        out_ref[at, :] += a[pl.ds(0, BLK), :].astype(F32)


def base(grad_pre, w_self, keeps, come, arrived):
    count, rows, width = keeps.shape
    slab = pl.BlockSpec((None, rows, width), lambda i: (count - 1, 0, 0))
    head = pl.BlockSpec((BLK + 16, width), lambda i: (0, 0))
    out = jax.ShapeDtypeStruct((rows, width), F32)
    return pl.pallas_call(
        partial(base_kernel, parts=len(come)),
        grid=(1,),
        in_specs=[spec(grad_pre), spec(w_self), slab]
        + [spec(x) for x in come]
        + [head] * len(arrived),
        out_specs=spec(out),
        out_shape=out,
        compiler_params=params(),
        cost_estimate=cost(4 * rows * width * width, 12 * rows * width),
        name="base",
    )(grad_pre, w_self, keeps, *come, *arrived)


def joined_kernel(*refs, more):
    out_ref = refs[-1]
    keep_ref, parts = refs[more], refs[more + 1 : -1]
    tall = parts[0].shape[0]
    for j, part in enumerate(parts):
        rows = pl.ds(j * tall, tall)
        total = keep_ref[rows, :].astype(F32) + part[...].astype(F32)
        if more:
            total = total + refs[0][rows, :].astype(F32)
        out_ref[rows, :] = total.astype(BF16)


def joined(got, keeps, come, s):
    _, rows, width = keeps.shape
    keep = pl.BlockSpec((None, rows, width), lambda i: (s, 0, 0))
    more = () if got is None else (got,)
    out = jax.ShapeDtypeStruct((rows, width), BF16)
    return pl.pallas_call(
        partial(joined_kernel, more=len(more)),
        grid=(1,),
        in_specs=[spec(x) for x in more] + [keep] + [spec(x) for x in come],
        out_specs=spec(out),
        out_shape=out,
        compiler_params=params(),
        cost_estimate=cost(3 * rows * width, 8 * rows * width),
        name=f"joined{s}",
    )(*more, keeps, *come)


def last_kernel(rest_ref, *refs):
    got, out_ref = refs[:-1], refs[-1]
    tall = got[0].shape[0]
    for j, ref in enumerate(got):
        rows = pl.ds(j * tall, tall)
        out_ref[rows, :] = rest_ref[rows, :] + ref[...].astype(F32)


def last(rest, got):
    def whole(x):
        return pl.BlockSpec(x.shape, lambda i: (0, 0))

    return pl.pallas_call(
        last_kernel,
        grid=(1,),
        in_specs=[whole(x) for x in (rest, *got)],
        out_specs=whole(rest),
        out_shape=jax.ShapeDtypeStruct(rest.shape, F32),
        compiler_params=params(),
        cost_estimate=cost(rest.size, 10 * rest.size),
        name="last",
    )(rest, *got)


def power(size):
    return size & (size - 1) == 0


def target(i, k, size):
    return i ^ k if power(size) else lax.rem(i + k, size)


def source(i, k, size):
    return i ^ k if power(size) else lax.rem(i + size - k, size)


def to_peer(x, axis, k):
    size = lax.axis_size(axis)
    return lax.ppermute(x, axis, [(i, i ^ k if power(size) else (i + k) % size) for i in range(size)])


def back_to(x, axis, k):
    size = lax.axis_size(axis)
    return to_peer(x, axis, k if power(size) else size - k)


def tree_sum(parts):
    while len(parts) > 1:
        pairs = [a + b for a, b in zip(parts[::2], parts[1::2])]
        parts = pairs + parts[len(pairs) * 2 :]
    return parts[0]


def shards(
    features,
    band_tiles,
    band_cols,
    off_tiles,
    req_block,
    req_row,
    req_valid,
    weight_self,
    weight_neigh,
    bias_term,
    cotangent,
):
    row_count, width = features.shape
    n = lax.axis_size("narrow")
    wide = lax.axis_size("wide")
    steps = n // 2
    fold = [0] + list(range(1, steps, 2)) + list(range(2, steps, 2))[::-1]
    after = {a: b for a, b in zip(fold, fold[1:] + fold[:1])}

    def onward(x):
        return lax.ppermute(x, "narrow", [(i, after[i // 2] * 2 + i % 2) for i in range(n)])

    def swap(x):
        return to_peer(x, "narrow", 1)

    me = lax.axis_index("narrow")
    here = lax.axis_index("wide")
    chips = jnp.array(
        [[fold[(fold.index(z) - s) % steps] for s in range(steps)] for z in range(steps)], jnp.int32
    )[me // 2]
    ids = jnp.concatenate([(me % 2)[None].astype(jnp.int32), chips])
    cols = band_cols.reshape(-1)
    asked, row, valid = req_block[0], req_row[0], req_valid[0]
    def tie(*xs):
        return lax.optimization_barrier(xs)

    def cut(x):
        tall = row_count // CHUNKS
        return [x] if CHUNKS == 1 else [lax.slice_in_dim(x, j * tall, (j + 1) * tall) for j in range(CHUNKS)]

    tiles = band_tiles
    slabs, pairs = [cut(features)], []
    asked_of_me = [asked] + [to_peer(asked, "wide", k) for k in range(1, wide)]
    sums = ()
    for s in range(1, steps):
        following = [onward(x) for x in slabs[-1]]
        pairs.append([swap(x) for x in slabs[-1]])
        off = (row, valid, off_tiles, fetched) if s == steps - 1 else ()
        sums = pull(ids, cols, tiles, slabs[-1], pairs[-1], sums, s - 1, off)
        following[-1], *sums = tie(following[-1], *sums)
        if s == 1:
            following[-1], *asked_of_me = tie(following[-1], *asked_of_me)
            served = serve(asked_of_me, features)
            fetched = [served[0]] + [back_to(served[k], "wide", k) for k in range(1, wide)]
        elif s == 2:
            following[-1], *fetched = tie(following[-1], *fetched)
        slabs.append(following)
        if s == steps - 2:
            halved = halve(tiles)
            halved, *sums = tie(halved, *sums)
    pairs.append([swap(x) for x in slabs[-1]])
    layer_out, grad_pre, aggregate, signal, keep, send = middle(
        ids, cols, halved, cotangent, sums, features, weight_self, weight_neigh,
        bias_term.reshape(1, -1), slabs[-1], pairs[-1], steps,
    )

    come = swap(send)
    keep2, send2 = push(ids, cols, signal, halved, (2 % steps,))
    mine, other, *pushed = grads(
        ids, asked, row, valid, off_tiles, signal, features, aggregate, grad_pre
    )
    come, mine, other, keep2, *more = tie(come, mine, other, keep2, *send2, *pushed)
    send2, pushed = more[: len(send2)], more[len(send2) :]
    got = onward(joined(None, keep[None], [come], 0))
    come2 = [swap(x) for x in send2]
    packed = pack(mine, swap(other), pushed)
    arrived = [packed[0]] + [to_peer(packed[k], "wide", k) for k in range(1, wide)]
    total = piece_sum(arrived)
    if not power(steps):
        total = lax.psum(total, "narrow", axis_index_groups=[list(range(c, n, 2)) for c in (0, 1)])
    later = tuple((s + 3) % steps for s in range(steps - 2))
    k = 1
    for s in range(steps - 2):
        if power(steps) and k < steps:
            total = total + to_peer(total, "narrow", 2 * k)
            k *= 2
        got, total = tie(got, total)
        if s == 0:
            got, signal = tie(got, signal)
            going = joined(got, keep2, come2, 0)
            keeps, sends = push(ids, cols, signal, halved, later)
            comes = [swap(x) for x in sends]
            rest = base(grad_pre, weight_self, keeps, comes[-PARTS:], arrived)
        else:
            if s == 1:
                got, rest = tie(got, rest)
            going = joined(got, keeps, comes[(s - 1) * PARTS : s * PARTS], s - 1)
        got = onward(going)
    while power(steps) and k < steps:
        total = total + to_peer(total, "narrow", 2 * k)
        k *= 2
    pieces = [total] + [to_peer(total, "wide", k) for k in range(1, wide)]
    whole = half(pieces, (wide * n * row_count) ** (-0.5))
    grad_self, grad_neigh, grad_bias = finish(ids, whole, swap(whole))
    got, grad_self, grad_neigh, grad_bias = tie(got, grad_self, grad_neigh, grad_bias)
    grad_features = last(rest, [got])
    return layer_out, grad_features, grad_self, grad_neigh, grad_bias.reshape(-1)


def solution(mesh):
    both = ("wide", "narrow")
    placed = (
        P(both, None),
        P(both, None, None, None),
        P(both, None),
        P(both, None, None, None),
        P(both, None),
        P(both, None),
        P(both, None),
        P(),
        P(),
        P(),
        P(both, None),
    )
    return jax.shard_map(
        shards,
        mesh=mesh,
        in_specs=placed,
        out_specs=(P(both, None), P(both, None), P(), P(), P()),
        check_vma=False,
    )
```

```python
from functools import partial

import jax
import jax.numpy as jnp
from jax import lax
from jax.experimental import pallas as pl
from jax.experimental.pallas import tpu as pltpu
from jax.sharding import PartitionSpec as P

F32 = jnp.float32
BF16 = jnp.bfloat16
BLK = 128
ROWS_PER = 4
CHUNKS = 2
PARTS = 2
VMEM = 28 * 1024 * 1024


def mm(a, b, lhs=1, rhs=0):
    return lax.dot_general(a, b, (((lhs,), (rhs,)), ((), ())), preferred_element_type=F32)


def params():
    return pltpu.CompilerParams(vmem_limit_bytes=VMEM)


def cost(flops, nbytes, trans=0):
    return pl.CostEstimate(flops=flops, bytes_accessed=nbytes, transcendentals=trans)


def fold_of(steps):
    return [0] + list(range(1, steps, 2)) + list(range(2, steps, 2))[::-1]


class Place:
    def __init__(self, n):
        me = lax.axis_index("narrow")
        self.core, self.chip, self.steps = lax.rem(me, 2), lax.div(me, 2), n // 2

    def at(self, s):
        fold = fold_of(self.steps)
        found = jnp.int32(0)
        for z in range(self.steps):
            found = jnp.where(self.chip == z, fold[(fold.index(z) - s) % self.steps], found)
        return found


def block(ref, index):
    return ref[pl.ds(pl.multiple_of(index * BLK, BLK), BLK), :]


def tile_reads(tiles_ref, buffer, sems, chip):
    count = buffer.shape[0] // ROWS_PER
    reads = []
    for q in range(count):
        rows = pl.ds(q * ROWS_PER, ROWS_PER)
        reads.append(
            pltpu.make_async_copy(
                tiles_ref.at[rows, pl.ds(chip * 2, 2)], buffer.at[rows], sems.at[q]
            )
        )
    for r in reads:
        r.start()
    return reads


def pair_sum(core, cols, pair, slabs_ref, g, n, chip, base=0):
    own = block(slabs_ref.at[0], cols[chip * 2 + core, g])
    sib = block(slabs_ref.at[1], cols[chip * 2 + 1 - core, g])
    mine, other = pair[g, base + core].astype(F32), pair[g, base + 1 - core].astype(F32)
    return mm(mine.astype(BF16), own) + mm(other.astype(BF16), sib), mine + other


def lay_out(parts, slabs_ref):
    at = 0
    for part in parts:
        half, row = divmod(at, slabs_ref.shape[1])
        slabs_ref[half, pl.ds(row, part.shape[0]), :] = part[...]
        at += part.shape[0]


def spec(x):
    return pl.BlockSpec(x.shape, lambda *i: (0,) * len(x.shape))


def in_hbm():
    return pl.BlockSpec(memory_space=pltpu.HBM)


def halve_kernel(t_ref, out_ref):
    out_ref[...] = t_ref[...].astype(F32).astype(BF16)


def halve(tiles):
    g, n = tiles.shape[:2]
    one = pl.BlockSpec((1, n, BLK, BLK), lambda i: (i, 0, 0, 0))
    return pl.pallas_call(
        halve_kernel,
        grid=(g,),
        in_specs=[one],
        out_specs=one,
        out_shape=jax.ShapeDtypeStruct(tiles.shape, BF16),
        compiler_params=params(),
        cost_estimate=cost(tiles.size, 6 * tiles.size),
        name="halve",
    )(tiles)


def pull_kernel(cols, *refs, n, step, chunks, wide):
    refs = list(refs)
    if wide:
        row, valid = refs[:2]
        refs = refs[2:]
    tiles_ref, parts = refs[0], refs[1 : 1 + chunks]
    refs = refs[1 + chunks :]
    if step:
        acc_in, counts_in = refs[:2]
        refs = refs[2:]
    if wide:
        off_ref, fetched = refs[0], refs[1 : 1 + wide]
        refs = refs[1 + wide :]
        here = lax.axis_index("wide")
    acc_ref, counts_ref, slabs_ref, pair, sems = refs[:5]
    here_now = Place(n)
    core, chip = here_now.core, here_now.at(step)
    reads = tile_reads(tiles_ref, pair, sems, chip)
    lay_out(parts, slabs_ref)
    for q, r in enumerate(reads):
        r.wait()
        for g in range(q * ROWS_PER, (q + 1) * ROWS_PER):
            rows = pl.ds(g * BLK, BLK)
            part, count = pair_sum(core, cols, pair, slabs_ref, g, n, chip)
            acc_ref[rows, :] = acc_in[rows, :] + part if step else part
            counts_ref[rows, :] = counts_in[rows, :] + count if step else count
    if wide:
        for k in range(wide):
            src = target(here, k, wide)
            mask = (off_ref[0, src] * valid[src]).astype(F32)
            at = pl.ds(pl.multiple_of(row[src] * BLK, BLK), BLK)
            acc_ref[at, :] += mm(mask.astype(BF16), fetched[k][...])
            counts_ref[at, :] += mask


def pull(cols, tiles, own, sib, sums, step, off=()):
    g, n = tiles.shape[:2]
    width = own[0].shape[1]
    rows = g * BLK
    wide = 0
    scalars, ins = [], [*own, *sib, *sums]
    specs = [in_hbm()] + [spec(x) for x in ins]
    if off:
        *scalars, off_tiles, fetched = off
        wide = len(fetched)
        ins += [off_tiles, *fetched]
        specs += [spec(x) for x in (off_tiles, *fetched)]
    out = jax.ShapeDtypeStruct((rows, width), F32)
    return pl.pallas_call(
        partial(pull_kernel, n=n, step=step, chunks=len(own) + len(sib), wide=wide),
        grid_spec=pltpu.PrefetchScalarGridSpec(
            num_scalar_prefetch=1 + len(scalars),
            grid=(1,),
            in_specs=specs,
            out_specs=[spec(out)] * 2,
            scratch_shapes=[
                pltpu.VMEM((2, rows, width), BF16),
                pltpu.VMEM((g, 2, BLK, BLK), jnp.int32),
                pltpu.SemaphoreType.DMA((g // ROWS_PER,)),
            ],
        ),
        out_shape=[out] * 2,
        compiler_params=params(),
        cost_estimate=cost(4 * rows * BLK * width, 12 * rows * width),
        name=f"pull{step}",
    )(cols, *scalars, tiles, *ins)


def serve_kernel(*refs, wide):
    asked, feat_ref, outs = refs[:wide], refs[wide], refs[wide + 1 :]
    here = lax.axis_index("wide")
    for k in range(wide):
        outs[k][...] = block(feat_ref, asked[k][here])


def serve(asked, features):
    wide = len(asked)
    out = jax.ShapeDtypeStruct((BLK, features.shape[1]), features.dtype)
    return pl.pallas_call(
        partial(serve_kernel, wide=wide),
        grid_spec=pltpu.PrefetchScalarGridSpec(
            num_scalar_prefetch=wide,
            grid=(1,),
            in_specs=[spec(features)],
            out_specs=[spec(out)] * wide,
        ),
        out_shape=[out] * wide,
        compiler_params=params(),
        cost_estimate=cost(0, 4 * features.size),
        name="serve",
    )(*asked, features)


def place(cols, tiles_ref, signal_rows, place_ref, g, core, chip, n):
    for j in range(2):
        which = core if j == 0 else 1 - core
        at = pl.ds(pl.multiple_of(cols[chip * 2 + which, g] * BLK, BLK), BLK)
        place_ref[j, at, :] += mm(tiles_ref[g, chip * 2 + which], signal_rows, 0, 0)


def middle_kernel(
    cols, tiles_ref, cot_ref, acc_ref, counts_ref, feat_ref, wself_ref, wneigh_ref, bias_ref,
    *refs, n, steps, chunks,
):
    parts, refs = refs[: 2 * chunks], refs[2 * chunks :]
    out_hbm, gp_ref, agg_ref, sig_ref, keep_ref, send_ref = refs[:6]
    place_ref, slabs_ref, out, out_sems = refs[6:]
    place_now = Place(n)
    core, last, first = place_now.core, place_now.at(steps - 1), place_now.at(1)
    tall = ROWS_PER * BLK
    count = feat_ref.shape[0] // tall

    def rows_of(q):
        return pl.ds(q * tall, tall)

    writes = [
        pltpu.make_async_copy(out.at[rows_of(q)], out_hbm.at[rows_of(q)], out_sems.at[q])
        for q in range(count)
    ]
    place_ref[...] = jnp.zeros_like(place_ref)
    lay_out(parts, slabs_ref)
    ones = jnp.ones((BLK, BLK), BF16)
    slope = 0.7978845608028654
    for q in range(count):
        rows = rows_of(q)
        both = [
            pair_sum(core, cols, tiles_ref, slabs_ref, g, n, last, last * 2)
            for g in range(q * ROWS_PER, (q + 1) * ROWS_PER)
        ]
        gathered = acc_ref[rows, :] + jnp.concatenate([b[0] for b in both], axis=0)
        counts = counts_ref[rows, :] + jnp.concatenate([b[1] for b in both], axis=0)
        inverse = 1.0 / (mm(counts.astype(BF16), ones) + 1.0)
        aggregate = (gathered * inverse).astype(BF16)
        agg_ref[rows, :] = aggregate
        pre = mm(feat_ref[rows, :], wself_ref[...]) + mm(aggregate, wneigh_ref[...])
        pre = pre + bias_ref[...].astype(F32)
        square = pre * pre
        bent = jnp.tanh(slope * (pre + 0.044715 * (square * pre)))
        half = 0.5 * (1.0 + bent)
        out[rows, :] = (pre * half).astype(BF16)
        writes[q].start()
        deriv = half + (0.5 * pre) * (1.0 - bent * bent) * (
            slope + (3 * 0.044715 * slope) * square
        )
        grad_pre = (cot_ref[rows, :].astype(F32) * deriv).astype(BF16)
        gp_ref[rows, :] = grad_pre
        signal = (mm(grad_pre, wneigh_ref[...], 1, 1) * inverse).astype(BF16)
        sig_ref[rows, :] = signal
        for b in range(ROWS_PER):
            rows_b = signal[b * BLK : (b + 1) * BLK]
            place(cols, tiles_ref, rows_b, place_ref, q * ROWS_PER + b, core, first, n)
    keep_ref[...] = place_ref[0].astype(BF16)
    send_ref[...] = place_ref[1].astype(BF16)
    for w in writes:
        w.wait()


def middle(cols, tiles, cot, sums, features, w_self, w_neigh, bias, own, sib, steps):
    g, n = tiles.shape[:2]
    rows, width = features.shape
    outw = w_self.shape[1]
    count = g // ROWS_PER

    def shape(c):
        return jax.ShapeDtypeStruct((rows, c), BF16)

    ins = (*sums, features, w_self, w_neigh, bias, *own, *sib)
    outs = [shape(outw), shape(outw), shape(width), shape(width), shape(width), shape(width)]
    return pl.pallas_call(
        partial(middle_kernel, n=n, steps=steps, chunks=len(own)),
        grid_spec=pltpu.PrefetchScalarGridSpec(
            num_scalar_prefetch=1,
            grid=(1,),
            in_specs=[spec(x) for x in (tiles, cot, *ins)],
            out_specs=[in_hbm()] + [spec(x) for x in outs[1:]],
            scratch_shapes=[
                pltpu.VMEM((2, rows, width), F32),
                pltpu.VMEM((2, rows, width), BF16),
                pltpu.VMEM((rows, outw), BF16),
                pltpu.SemaphoreType.DMA((count,)),
            ],
        ),
        out_shape=outs,
        compiler_params=params(),
        cost_estimate=cost(
            8 * rows * BLK * width + 6 * rows * width * outw, 30 * rows * width, rows * outw
        ),
        name="middle",
    )(cols, tiles, cot, *ins)


def push_kernel(cols, tiles_ref, sig_ref, keep_ref, *refs, n, which):
    *send_refs, place_ref = refs
    now = Place(n)
    parts = len(send_refs) // len(which)
    tall = send_refs[0].shape[0]
    for p, s in enumerate(which):
        place_ref[...] = jnp.zeros_like(place_ref)
        for g in range(tiles_ref.shape[0]):
            rows = sig_ref[g * BLK : (g + 1) * BLK, :]
            place(cols, tiles_ref, rows, place_ref, g, now.core, now.at(s), n)
        keep_ref[p] = place_ref[0].astype(BF16)
        for j in range(parts):
            send_refs[p * parts + j][...] = place_ref[1, pl.ds(j * tall, tall), :].astype(BF16)


def push(cols, signal, tiles, which):
    g, n = tiles.shape[:2]
    rows, width = signal.shape
    count = len(which)
    outs = [jax.ShapeDtypeStruct((count, rows, width), BF16)]
    outs += [jax.ShapeDtypeStruct((rows // PARTS, width), BF16)] * (count * PARTS)
    keeps, *sends = pl.pallas_call(
        partial(push_kernel, n=n, which=which),
        grid_spec=pltpu.PrefetchScalarGridSpec(
            num_scalar_prefetch=1,
            grid=(1,),
            in_specs=[spec(tiles), spec(signal)],
            out_specs=[spec(x) for x in outs],
            scratch_shapes=[pltpu.VMEM((2, rows, width), F32)],
        ),
        out_shape=outs,
        compiler_params=params(),
        cost_estimate=cost(4 * count * rows * BLK * width, 8 * count * rows * width),
        name="push",
    )(cols, tiles, signal)
    return keeps, sends


def half_rows(wide):
    step = 16 * wide
    return (BLK + 1 + step - 1) // step * step


def grads_kernel(
    asked, row, valid, off_ref, sig_ref, feat_ref, agg_ref, gp_ref,
    mine_ref, other_ref, *pushed_refs, wide,
):
    here = lax.axis_index("wide")
    tall = 4 * BLK
    dself = dneigh = dbias = None
    for i in range(feat_ref.shape[0] // tall):
        rows = pl.ds(i * tall, tall)
        gp = gp_ref[rows, :]
        a = mm(feat_ref[rows, :], gp, 0, 0)
        b = mm(agg_ref[rows, :], gp, 0, 0)
        c = jnp.sum(gp.astype(F32), axis=0, keepdims=True)
        dself, dneigh, dbias = (a, b, c) if i == 0 else (dself + a, dneigh + b, dbias + c)
    first = lax.rem(lax.axis_index("narrow"), 2) == 0
    mine_ref[pl.ds(0, BLK), :] = jnp.where(first, dself, dneigh)
    other_ref[pl.ds(0, BLK), :] = jnp.where(first, dneigh, dself)
    spare = mine_ref.shape[0] - BLK
    mine_ref[pl.ds(BLK, spare), :] = jnp.broadcast_to(dbias, (spare, dbias.shape[1]))
    other_ref[pl.ds(BLK, spare), :] = jnp.broadcast_to(dbias, (spare, dbias.shape[1]))
    for k in range(wide):
        peer = target(here, k, wide)
        mask = (off_ref[0, peer] * valid[peer]).astype(F32).astype(BF16)
        at = pl.ds(pl.multiple_of(row[peer] * BLK, BLK), BLK)
        ref = pushed_refs[k]
        ref[pl.ds(0, BLK), :] = mm(mask, sig_ref[at, :], 0, 0).astype(BF16)
        ref[pl.ds(BLK, 16), :] = jnp.full((16, BLK), asked[peer], jnp.int32).astype(F32).astype(BF16)


def grads(asked, row, valid, off_tiles, signal, features, aggregate, grad_pre):
    wide = off_tiles.shape[1]
    rows, width = features.shape
    outw = grad_pre.shape[1]

    def whole(x):
        return pl.BlockSpec(x.shape, lambda i, *s: (0,) * len(x.shape))

    ins = (off_tiles, signal, features, aggregate, grad_pre)
    outs = [jax.ShapeDtypeStruct((half_rows(wide), outw), F32)] * 2
    outs += [jax.ShapeDtypeStruct((BLK + 16, width), BF16)] * wide
    return pl.pallas_call(
        partial(grads_kernel, wide=wide),
        grid_spec=pltpu.PrefetchScalarGridSpec(
            num_scalar_prefetch=3,
            grid=(1,),
            in_specs=[whole(x) for x in ins],
            out_specs=[whole(x) for x in outs],
        ),
        out_shape=outs,
        compiler_params=params(),
        cost_estimate=cost(8 * rows * width * width, 16 * rows * width),
        name="grads",
    )(asked, row, valid, *ins)


def pack_kernel(mine_ref, come_ref, *refs, wide):
    pushed_refs, msg_refs = refs[:wide], refs[wide:]
    here = lax.axis_index("wide")
    piece = mine_ref.shape[0] // wide
    head = BLK + 16
    for k in range(wide):
        peer = target(here, k, wide)
        rows = pl.ds(pl.multiple_of(peer * piece, 16), piece)
        total = mine_ref[rows, :] + come_ref[rows, :]
        high = total.astype(BF16)
        low = (total - high.astype(F32)).astype(BF16)
        msg_refs[k][pl.ds(0, head), :] = pushed_refs[k][...]
        for j, x in enumerate((high[:, :BLK], high[:, BLK:], low[:, :BLK], low[:, BLK:])):
            msg_refs[k][pl.ds(head + j * piece, piece), :] = x


def pack(mine, come, pushed):
    wide = len(pushed)

    def whole(x):
        return pl.BlockSpec(x.shape, lambda i: (0,) * len(x.shape))

    ins = (mine, come, *pushed)
    tall = BLK + 16 + mine.shape[0] // wide * 4
    outs = [jax.ShapeDtypeStruct((tall, pushed[0].shape[1]), BF16)] * wide
    return pl.pallas_call(
        partial(pack_kernel, wide=wide),
        grid=(1,),
        in_specs=[whole(x) for x in ins],
        out_specs=[whole(x) for x in outs],
        out_shape=outs,
        compiler_params=params(),
        cost_estimate=cost(4 * mine.size, 20 * mine.size),
        name="pack",
    )(*ins)


def piece_sum_kernel(*refs):
    arrived, out_ref = refs[:-1], refs[-1]
    piece = out_ref.shape[0]
    head = BLK + 16
    for side in range(2):
        part = [
            a[pl.ds(head + side * piece, piece), :].astype(F32)
            + a[pl.ds(head + (side + 2) * piece, piece), :].astype(F32)
            for a in arrived
        ]
        out_ref[:, pl.ds(side * BLK, BLK)] = tree_sum(part)


def piece_sum(arrived):
    def whole(x):
        return pl.BlockSpec(x.shape, lambda i: (0,) * len(x.shape))

    piece = (arrived[0].shape[0] - BLK - 16) // 4
    out = jax.ShapeDtypeStruct((piece, 2 * BLK), F32)
    return pl.pallas_call(
        piece_sum_kernel,
        grid=(1,),
        in_specs=[whole(x) for x in arrived],
        out_specs=whole(out),
        out_shape=out,
        compiler_params=params(),
        cost_estimate=cost(arrived[0].size * len(arrived), 2 * arrived[0].size * len(arrived)),
        name="piece_sum",
    )(*arrived)


def half_kernel(*refs, factor):
    pieces, out_ref = refs[:-1], refs[-1]
    wide, piece = len(pieces), pieces[0].shape[0]
    here = lax.axis_index("wide")
    for k in range(wide):
        at = pl.ds(pl.multiple_of(source(here, k, wide) * piece, 16), piece)
        out_ref[at, :] = pieces[k][...] * factor


def half(pieces, factor):
    def whole(x):
        return pl.BlockSpec(x.shape, lambda i: (0, 0))

    out = jax.ShapeDtypeStruct((pieces[0].shape[0] * len(pieces), pieces[0].shape[1]), F32)
    return pl.pallas_call(
        partial(half_kernel, factor=factor),
        grid=(1,),
        in_specs=[whole(x) for x in pieces],
        out_specs=whole(out),
        out_shape=out,
        compiler_params=params(),
        cost_estimate=cost(out.size, 8 * out.size),
        name="half",
    )(*pieces)


def finish_kernel(total_ref, paired_ref, self_ref, neigh_ref, bias_ref):
    first = lax.rem(lax.axis_index("narrow"), 2) == 0
    total, paired = total_ref[pl.ds(0, BLK), :], paired_ref[pl.ds(0, BLK), :]
    self_ref[...] = jnp.where(first, total, paired)
    neigh_ref[...] = jnp.where(first, paired, total)
    at = pl.ds(BLK, 8)
    bias_ref[...] = jnp.where(first, total_ref[at, :], paired_ref[at, :])[:1]


def finish(total, paired):
    def whole(x):
        return pl.BlockSpec(x.shape, lambda i, *s: (0, 0))

    outs = [jax.ShapeDtypeStruct((r, 2 * BLK), F32) for r in (BLK, BLK, 1)]
    return pl.pallas_call(
        finish_kernel,
        grid=(1,),
        in_specs=[whole(total), whole(paired)],
        out_specs=[whole(x) for x in outs],
        out_shape=outs,
        compiler_params=params(),
        cost_estimate=cost(4 * total.size, 16 * total.size),
        name="finish",
    )(total, paired)


def base_kernel(gp_ref, wself_ref, keep_ref, *refs, parts):
    come, arrived, out_ref = refs[:parts], refs[parts:-1], refs[-1]
    tall = 4 * BLK
    for i in range(out_ref.shape[0] // tall):
        rows = pl.ds(i * tall, tall)
        out_ref[rows, :] = mm(gp_ref[rows, :], wself_ref[...], 1, 1) + keep_ref[rows, :].astype(F32)
    tall = come[0].shape[0]
    for j, part in enumerate(come):
        out_ref[pl.ds(j * tall, tall), :] += part[...].astype(F32)
    line = lax.broadcasted_iota(jnp.int32, (16, BLK), 0)
    for a in arrived:
        index = jnp.max(jnp.where(line == 0, a[pl.ds(BLK, 16), :].astype(F32), 0.0))
        at = pl.ds(pl.multiple_of(index.astype(jnp.int32) * BLK, BLK), BLK)
        out_ref[at, :] += a[pl.ds(0, BLK), :].astype(F32)


def base(grad_pre, w_self, keeps, come, arrived):
    count, rows, width = keeps.shape
    slab = pl.BlockSpec((None, rows, width), lambda i: (count - 1, 0, 0))
    head = pl.BlockSpec((BLK + 16, width), lambda i: (0, 0))
    out = jax.ShapeDtypeStruct((rows, width), F32)
    return pl.pallas_call(
        partial(base_kernel, parts=len(come)),
        grid=(1,),
        in_specs=[spec(grad_pre), spec(w_self), slab]
        + [spec(x) for x in come]
        + [head] * len(arrived),
        out_specs=spec(out),
        out_shape=out,
        compiler_params=params(),
        cost_estimate=cost(4 * rows * width * width, 12 * rows * width),
        name="base",
    )(grad_pre, w_self, keeps, *come, *arrived)


def joined_kernel(*refs, more):
    out_ref = refs[-1]
    keep_ref, parts = refs[more], refs[more + 1 : -1]
    tall = parts[0].shape[0]
    for j, part in enumerate(parts):
        rows = pl.ds(j * tall, tall)
        total = keep_ref[rows, :].astype(F32) + part[...].astype(F32)
        if more:
            total = total + refs[0][rows, :].astype(F32)
        out_ref[rows, :] = total.astype(BF16)


def joined(got, keeps, come, s):
    _, rows, width = keeps.shape
    keep = pl.BlockSpec((None, rows, width), lambda i: (s, 0, 0))
    more = () if got is None else (got,)
    out = jax.ShapeDtypeStruct((rows, width), BF16)
    return pl.pallas_call(
        partial(joined_kernel, more=len(more)),
        grid=(1,),
        in_specs=[spec(x) for x in more] + [keep] + [spec(x) for x in come],
        out_specs=spec(out),
        out_shape=out,
        compiler_params=params(),
        cost_estimate=cost(3 * rows * width, 8 * rows * width),
        name=f"joined{s}",
    )(*more, keeps, *come)


def last_kernel(rest_ref, *refs):
    got, out_ref = refs[:-1], refs[-1]
    tall = got[0].shape[0]
    for j, ref in enumerate(got):
        rows = pl.ds(j * tall, tall)
        out_ref[rows, :] = rest_ref[rows, :] + ref[...].astype(F32)


def last(rest, got):
    def whole(x):
        return pl.BlockSpec(x.shape, lambda i: (0, 0))

    return pl.pallas_call(
        last_kernel,
        grid=(1,),
        in_specs=[whole(x) for x in (rest, *got)],
        out_specs=whole(rest),
        out_shape=jax.ShapeDtypeStruct(rest.shape, F32),
        compiler_params=params(),
        cost_estimate=cost(rest.size, 10 * rest.size),
        name="last",
    )(rest, *got)


def power(size):
    return size & (size - 1) == 0


def target(i, k, size):
    return i ^ k if power(size) else lax.rem(i + k, size)


def source(i, k, size):
    return i ^ k if power(size) else lax.rem(i + size - k, size)


def to_peer(x, axis, k):
    size = lax.axis_size(axis)
    return lax.ppermute(x, axis, [(i, i ^ k if power(size) else (i + k) % size) for i in range(size)])


def back_to(x, axis, k):
    size = lax.axis_size(axis)
    return to_peer(x, axis, k if power(size) else size - k)


def tree_sum(parts):
    while len(parts) > 1:
        pairs = [a + b for a, b in zip(parts[::2], parts[1::2])]
        parts = pairs + parts[len(pairs) * 2 :]
    return parts[0]


def shards(
    features,
    band_tiles,
    band_cols,
    off_tiles,
    req_block,
    req_row,
    req_valid,
    weight_self,
    weight_neigh,
    bias_term,
    cotangent,
):
    row_count, width = features.shape
    n = lax.axis_size("narrow")
    wide = lax.axis_size("wide")
    steps = n // 2
    fold = fold_of(steps)
    after = {a: b for a, b in zip(fold, fold[1:] + fold[:1])}

    def onward(x):
        return lax.ppermute(x, "narrow", [(i, after[i // 2] * 2 + i % 2) for i in range(n)])

    def swap(x):
        return to_peer(x, "narrow", 1)

    cols = band_cols.T
    asked, row, valid = req_block[0], req_row[0], req_valid[0]
    def tie(*xs):
        return lax.optimization_barrier(xs)

    def cut(x):
        tall = row_count // CHUNKS
        return [x] if CHUNKS == 1 else [lax.slice_in_dim(x, j * tall, (j + 1) * tall) for j in range(CHUNKS)]

    tiles = band_tiles
    slabs, pairs = [cut(features)], []
    asked_of_me = [asked] + [to_peer(asked, "wide", k) for k in range(1, wide)]
    sums = ()
    for s in range(1, steps):
        following = [onward(x) for x in slabs[-1]]
        pairs.append([swap(features)] if s == 1 else [swap(x) for x in slabs[-1]])
        off = (row, valid, off_tiles, fetched) if s == steps - 1 else ()
        sums = pull(cols, tiles, slabs[-1], pairs[-1], sums, s - 1, off)
        at = 0 if s == 1 else -1
        following[at], *sums = tie(following[at], *sums)
        if s == 1:
            following[-1], *asked_of_me = tie(following[-1], *asked_of_me)
            served = serve(asked_of_me, features)
            fetched = [served[0]] + [back_to(served[k], "wide", k) for k in range(1, wide)]
        elif s == 2:
            following[-1], *fetched = tie(following[-1], *fetched)
        slabs.append(following)
        if s == steps - 2:
            halved = halve(tiles)
            halved, *sums = tie(halved, *sums)
    early = [swap(x) for x in slabs[-1][:-1]]
    slabs[-1][-1], *early = tie(slabs[-1][-1], *early)
    pairs.append([*early, swap(slabs[-1][-1])])
    layer_out, grad_pre, aggregate, signal, keep, send = middle(
        cols, halved, cotangent, sums, features, weight_self, weight_neigh,
        bias_term.reshape(1, -1), slabs[-1], pairs[-1], steps,
    )

    come = swap(send)
    keep2, send2 = push(cols, signal, halved, (2 % steps,))
    mine, other, *pushed = grads(
        asked, row, valid, off_tiles, signal, features, aggregate, grad_pre
    )
    come, mine, other, keep2, *more = tie(come, mine, other, keep2, *send2, *pushed)
    send2, pushed = more[: len(send2)], more[len(send2) :]
    got = onward(joined(None, keep[None], [come], 0))
    come2 = [swap(x) for x in send2]
    packed = pack(mine, swap(other), pushed)
    arrived = [packed[0]] + [to_peer(packed[k], "wide", k) for k in range(1, wide)]
    total = piece_sum(arrived)
    if not power(steps):
        total = lax.psum(total, "narrow", axis_index_groups=[list(range(c, n, 2)) for c in (0, 1)])
    later = tuple((s + 3) % steps for s in range(steps - 2))
    k = 1
    for s in range(steps - 2):
        if power(steps) and k < steps:
            total = total + to_peer(total, "narrow", 2 * k)
            k *= 2
        got, total = tie(got, total)
        if s == 0:
            got, signal = tie(got, signal)
            going = joined(got, keep2, come2, 0)
            keeps, sends = push(cols, signal, halved, later)
            comes = [swap(x) for x in sends]
            rest = base(grad_pre, weight_self, keeps, comes[-PARTS:], arrived)
        else:
            if s == 1:
                got, rest = tie(got, rest)
            going = joined(got, keeps, comes[(s - 1) * PARTS : s * PARTS], s - 1)
        got = onward(going)
    while power(steps) and k < steps:
        total = total + to_peer(total, "narrow", 2 * k)
        k *= 2
    pieces = [total] + [to_peer(total, "wide", k) for k in range(1, wide)]
    whole = half(pieces, (wide * n * row_count) ** (-0.5))
    grad_self, grad_neigh, grad_bias = finish(whole, swap(whole))
    got, grad_self, grad_neigh, grad_bias = tie(got, grad_self, grad_neigh, grad_bias)
    grad_features = last(rest, [got])
    return layer_out, grad_features, grad_self, grad_neigh, grad_bias.reshape(-1)


def solution(mesh):
    both = ("wide", "narrow")
    placed = (
        P(both, None),
        P(both, None, None, None),
        P(both, None),
        P(both, None, None, None),
        P(both, None),
        P(both, None),
        P(both, None),
        P(),
        P(),
        P(),
        P(both, None),
    )
    return jax.shard_map(
        shards,
        mesh=mesh,
        in_specs=placed,
        out_specs=(P(both, None), P(both, None), P(), P(), P()),
        check_vma=False,
    )
```

```python
from functools import partial

import jax
import jax.numpy as jnp
from jax import lax
from jax.experimental import pallas as pl
from jax.experimental.pallas import tpu as pltpu
from jax.sharding import PartitionSpec as P

F32 = jnp.float32
BF16 = jnp.bfloat16
BLK = 128
ROWS_PER = 4
CHUNKS = 2
PARTS = 2
SUM_CHUNKS = 2
VMEM = 28 * 1024 * 1024


def mm(a, b, lhs=1, rhs=0):
    return lax.dot_general(a, b, (((lhs,), (rhs,)), ((), ())), preferred_element_type=F32)


def params():
    return pltpu.CompilerParams(vmem_limit_bytes=VMEM)


def cost(flops, nbytes, trans=0):
    return pl.CostEstimate(flops=flops, bytes_accessed=nbytes, transcendentals=trans)


def fold_of(steps):
    return [0] + list(range(1, steps, 2)) + list(range(2, steps, 2))[::-1]


class Place:
    def __init__(self, n):
        me = lax.axis_index("narrow")
        self.core, self.chip, self.steps = lax.rem(me, 2), lax.div(me, 2), n // 2

    def at(self, s):
        fold = fold_of(self.steps)
        found = jnp.int32(0)
        for z in range(self.steps):
            found = jnp.where(self.chip == z, fold[(fold.index(z) - s) % self.steps], found)
        return found


def block(ref, index):
    return ref[pl.ds(pl.multiple_of(index * BLK, BLK), BLK), :]


def tile_reads(tiles_ref, buffer, sems, chip):
    count = buffer.shape[0] // ROWS_PER
    reads = []
    for q in range(count):
        rows = pl.ds(q * ROWS_PER, ROWS_PER)
        reads.append(
            pltpu.make_async_copy(
                tiles_ref.at[rows, pl.ds(chip * 2, 2)], buffer.at[rows], sems.at[q]
            )
        )
    for r in reads:
        r.start()
    return reads


def pair_sum(core, cols, pair, slabs_ref, g, n, chip, base=0):
    own = block(slabs_ref.at[0], cols[chip * 2 + core, g])
    sib = block(slabs_ref.at[1], cols[chip * 2 + 1 - core, g])
    mine, other = pair[g, base + core].astype(F32), pair[g, base + 1 - core].astype(F32)
    return mm(mine.astype(BF16), own) + mm(other.astype(BF16), sib), mine + other


def lay_out(parts, slabs_ref):
    at = 0
    for part in parts:
        half, row = divmod(at, slabs_ref.shape[1])
        slabs_ref[half, pl.ds(row, part.shape[0]), :] = part[...]
        at += part.shape[0]


def spec(x):
    return pl.BlockSpec(x.shape, lambda *i: (0,) * len(x.shape))


def in_hbm():
    return pl.BlockSpec(memory_space=pltpu.HBM)


def halve_kernel(t_ref, out_ref):
    out_ref[...] = t_ref[...].astype(F32).astype(BF16)


def halve(tiles):
    g, n = tiles.shape[:2]
    one = pl.BlockSpec((1, n, BLK, BLK), lambda i: (i, 0, 0, 0))
    return pl.pallas_call(
        halve_kernel,
        grid=(g,),
        in_specs=[one],
        out_specs=one,
        out_shape=jax.ShapeDtypeStruct(tiles.shape, BF16),
        compiler_params=params(),
        cost_estimate=cost(tiles.size, 6 * tiles.size),
        name="halve",
    )(tiles)


def pull_kernel(cols, *refs, n, step, chunks, wide):
    refs = list(refs)
    if wide:
        row, valid = refs[:2]
        refs = refs[2:]
    tiles_ref, parts = refs[0], refs[1 : 1 + chunks]
    refs = refs[1 + chunks :]
    if step:
        acc_in, counts_in = refs[:2]
        refs = refs[2:]
    if wide:
        off_ref, fetched = refs[0], refs[1 : 1 + wide]
        refs = refs[1 + wide :]
        here = lax.axis_index("wide")
    acc_ref, counts_ref, slabs_ref, pair, sems = refs[:5]
    here_now = Place(n)
    core, chip = here_now.core, here_now.at(step)
    reads = tile_reads(tiles_ref, pair, sems, chip)
    lay_out(parts, slabs_ref)
    for q, r in enumerate(reads):
        r.wait()
        for g in range(q * ROWS_PER, (q + 1) * ROWS_PER):
            rows = pl.ds(g * BLK, BLK)
            part, count = pair_sum(core, cols, pair, slabs_ref, g, n, chip)
            acc_ref[rows, :] = acc_in[rows, :] + part if step else part
            counts_ref[rows, :] = counts_in[rows, :] + count if step else count
    if wide:
        for k in range(wide):
            src = target(here, k, wide)
            mask = (off_ref[0, src] * valid[src]).astype(F32)
            at = pl.ds(pl.multiple_of(row[src] * BLK, BLK), BLK)
            acc_ref[at, :] += mm(mask.astype(BF16), fetched[k][...])
            counts_ref[at, :] += mask


def pull(cols, tiles, own, sib, sums, step, off=()):
    g, n = tiles.shape[:2]
    width = own[0].shape[1]
    rows = g * BLK
    wide = 0
    scalars, ins = [], [*own, *sib, *sums]
    specs = [in_hbm()] + [spec(x) for x in ins]
    if off:
        *scalars, off_tiles, fetched = off
        wide = len(fetched)
        ins += [off_tiles, *fetched]
        specs += [spec(x) for x in (off_tiles, *fetched)]
    out = jax.ShapeDtypeStruct((rows, width), F32)
    return pl.pallas_call(
        partial(pull_kernel, n=n, step=step, chunks=len(own) + len(sib), wide=wide),
        grid_spec=pltpu.PrefetchScalarGridSpec(
            num_scalar_prefetch=1 + len(scalars),
            grid=(1,),
            in_specs=specs,
            out_specs=[spec(out)] * 2,
            scratch_shapes=[
                pltpu.VMEM((2, rows, width), BF16),
                pltpu.VMEM((g, 2, BLK, BLK), jnp.int32),
                pltpu.SemaphoreType.DMA((g // ROWS_PER,)),
            ],
        ),
        out_shape=[out] * 2,
        compiler_params=params(),
        cost_estimate=cost(4 * rows * BLK * width, 12 * rows * width),
        name=f"pull{step}",
    )(cols, *scalars, tiles, *ins)


def serve_kernel(*refs, wide):
    asked, feat_ref, outs = refs[:wide], refs[wide], refs[wide + 1 :]
    here = lax.axis_index("wide")
    for k in range(wide):
        outs[k][...] = block(feat_ref, asked[k][here])


def serve(asked, features):
    wide = len(asked)
    out = jax.ShapeDtypeStruct((BLK, features.shape[1]), features.dtype)
    return pl.pallas_call(
        partial(serve_kernel, wide=wide),
        grid_spec=pltpu.PrefetchScalarGridSpec(
            num_scalar_prefetch=wide,
            grid=(1,),
            in_specs=[spec(features)],
            out_specs=[spec(out)] * wide,
        ),
        out_shape=[out] * wide,
        compiler_params=params(),
        cost_estimate=cost(0, 4 * features.size),
        name="serve",
    )(*asked, features)


def place(cols, tiles_ref, signal_rows, place_ref, g, core, chip, n):
    for j in range(2):
        which = core if j == 0 else 1 - core
        at = pl.ds(pl.multiple_of(cols[chip * 2 + which, g] * BLK, BLK), BLK)
        place_ref[j, at, :] += mm(tiles_ref[g, chip * 2 + which], signal_rows, 0, 0)


def middle_kernel(
    cols, tiles_ref, cot_ref, acc_ref, counts_ref, feat_ref, wself_ref, wneigh_ref, bias_ref,
    *refs, n, steps, chunks,
):
    parts, refs = refs[: 2 * chunks], refs[2 * chunks :]
    out_hbm, gp_ref, agg_ref, sig_ref, keep_ref, send_ref = refs[:6]
    place_ref, slabs_ref, out, out_sems = refs[6:]
    place_now = Place(n)
    core, last, first = place_now.core, place_now.at(steps - 1), place_now.at(1)
    tall = ROWS_PER * BLK
    count = feat_ref.shape[0] // tall

    def rows_of(q):
        return pl.ds(q * tall, tall)

    writes = [
        pltpu.make_async_copy(out.at[rows_of(q)], out_hbm.at[rows_of(q)], out_sems.at[q])
        for q in range(count)
    ]
    place_ref[...] = jnp.zeros_like(place_ref)
    lay_out(parts, slabs_ref)
    ones = jnp.ones((BLK, BLK), BF16)
    slope = 0.7978845608028654
    for q in range(count):
        rows = rows_of(q)
        both = [
            pair_sum(core, cols, tiles_ref, slabs_ref, g, n, last, last * 2)
            for g in range(q * ROWS_PER, (q + 1) * ROWS_PER)
        ]
        gathered = acc_ref[rows, :] + jnp.concatenate([b[0] for b in both], axis=0)
        counts = counts_ref[rows, :] + jnp.concatenate([b[1] for b in both], axis=0)
        inverse = 1.0 / (mm(counts.astype(BF16), ones) + 1.0)
        aggregate = (gathered * inverse).astype(BF16)
        agg_ref[rows, :] = aggregate
        pre = mm(feat_ref[rows, :], wself_ref[...]) + mm(aggregate, wneigh_ref[...])
        pre = pre + bias_ref[...].astype(F32)
        square = pre * pre
        bent = jnp.tanh(slope * (pre + 0.044715 * (square * pre)))
        half = 0.5 * (1.0 + bent)
        out[rows, :] = (pre * half).astype(BF16)
        writes[q].start()
        deriv = half + (0.5 * pre) * (1.0 - bent * bent) * (
            slope + (3 * 0.044715 * slope) * square
        )
        grad_pre = (cot_ref[rows, :].astype(F32) * deriv).astype(BF16)
        gp_ref[rows, :] = grad_pre
        signal = (mm(grad_pre, wneigh_ref[...], 1, 1) * inverse).astype(BF16)
        sig_ref[rows, :] = signal
        for b in range(ROWS_PER):
            rows_b = signal[b * BLK : (b + 1) * BLK]
            place(cols, tiles_ref, rows_b, place_ref, q * ROWS_PER + b, core, first, n)
    keep_ref[...] = place_ref[0].astype(BF16)
    send_ref[...] = place_ref[1].astype(BF16)
    for w in writes:
        w.wait()


def middle(cols, tiles, cot, sums, features, w_self, w_neigh, bias, own, sib, steps):
    g, n = tiles.shape[:2]
    rows, width = features.shape
    outw = w_self.shape[1]
    count = g // ROWS_PER

    def shape(c):
        return jax.ShapeDtypeStruct((rows, c), BF16)

    ins = (*sums, features, w_self, w_neigh, bias, *own, *sib)
    outs = [shape(outw), shape(outw), shape(width), shape(width), shape(width), shape(width)]
    return pl.pallas_call(
        partial(middle_kernel, n=n, steps=steps, chunks=len(own)),
        grid_spec=pltpu.PrefetchScalarGridSpec(
            num_scalar_prefetch=1,
            grid=(1,),
            in_specs=[spec(x) for x in (tiles, cot, *ins)],
            out_specs=[in_hbm()] + [spec(x) for x in outs[1:]],
            scratch_shapes=[
                pltpu.VMEM((2, rows, width), F32),
                pltpu.VMEM((2, rows, width), BF16),
                pltpu.VMEM((rows, outw), BF16),
                pltpu.SemaphoreType.DMA((count,)),
            ],
        ),
        out_shape=outs,
        compiler_params=params(),
        cost_estimate=cost(
            8 * rows * BLK * width + 6 * rows * width * outw, 30 * rows * width, rows * outw
        ),
        name="middle",
    )(cols, tiles, cot, *ins)


def push_kernel(cols, tiles_ref, sig_ref, keep_ref, *refs, n, which):
    *send_refs, place_ref = refs
    now = Place(n)
    parts = len(send_refs) // len(which)
    tall = send_refs[0].shape[0]
    for p, s in enumerate(which):
        place_ref[...] = jnp.zeros_like(place_ref)
        for g in range(tiles_ref.shape[0]):
            rows = sig_ref[g * BLK : (g + 1) * BLK, :]
            place(cols, tiles_ref, rows, place_ref, g, now.core, now.at(s), n)
        keep_ref[p] = place_ref[0].astype(BF16)
        for j in range(parts):
            send_refs[p * parts + j][...] = place_ref[1, pl.ds(j * tall, tall), :].astype(BF16)


def push(cols, signal, tiles, which):
    g, n = tiles.shape[:2]
    rows, width = signal.shape
    count = len(which)
    outs = [jax.ShapeDtypeStruct((count, rows, width), BF16)]
    outs += [jax.ShapeDtypeStruct((rows // PARTS, width), BF16)] * (count * PARTS)
    keeps, *sends = pl.pallas_call(
        partial(push_kernel, n=n, which=which),
        grid_spec=pltpu.PrefetchScalarGridSpec(
            num_scalar_prefetch=1,
            grid=(1,),
            in_specs=[spec(tiles), spec(signal)],
            out_specs=[spec(x) for x in outs],
            scratch_shapes=[pltpu.VMEM((2, rows, width), F32)],
        ),
        out_shape=outs,
        compiler_params=params(),
        cost_estimate=cost(4 * count * rows * BLK * width, 8 * count * rows * width),
        name="push",
    )(cols, tiles, signal)
    return keeps, sends


def half_rows(wide):
    step = 16 * wide
    return (BLK + 1 + step - 1) // step * step


def grads_kernel(
    asked, row, valid, off_ref, sig_ref, feat_ref, agg_ref, gp_ref,
    mine_ref, other_ref, *pushed_refs, wide,
):
    here = lax.axis_index("wide")
    tall = 4 * BLK
    dself = dneigh = dbias = None
    for i in range(feat_ref.shape[0] // tall):
        rows = pl.ds(i * tall, tall)
        gp = gp_ref[rows, :]
        a = mm(feat_ref[rows, :], gp, 0, 0)
        b = mm(agg_ref[rows, :], gp, 0, 0)
        c = jnp.sum(gp.astype(F32), axis=0, keepdims=True)
        dself, dneigh, dbias = (a, b, c) if i == 0 else (dself + a, dneigh + b, dbias + c)
    first = lax.rem(lax.axis_index("narrow"), 2) == 0
    mine_ref[pl.ds(0, BLK), :] = jnp.where(first, dself, dneigh)
    other_ref[pl.ds(0, BLK), :] = jnp.where(first, dneigh, dself)
    spare = mine_ref.shape[0] - BLK
    mine_ref[pl.ds(BLK, spare), :] = jnp.broadcast_to(dbias, (spare, dbias.shape[1]))
    other_ref[pl.ds(BLK, spare), :] = jnp.broadcast_to(dbias, (spare, dbias.shape[1]))
    for k in range(wide):
        peer = target(here, k, wide)
        mask = (off_ref[0, peer] * valid[peer]).astype(F32).astype(BF16)
        at = pl.ds(pl.multiple_of(row[peer] * BLK, BLK), BLK)
        ref = pushed_refs[k]
        ref[pl.ds(0, BLK), :] = mm(mask, sig_ref[at, :], 0, 0).astype(BF16)
        ref[pl.ds(BLK, 16), :] = jnp.full((16, BLK), asked[peer], jnp.int32).astype(F32).astype(BF16)


def grads(asked, row, valid, off_tiles, signal, features, aggregate, grad_pre):
    wide = off_tiles.shape[1]
    rows, width = features.shape
    outw = grad_pre.shape[1]

    def whole(x):
        return pl.BlockSpec(x.shape, lambda i, *s: (0,) * len(x.shape))

    ins = (off_tiles, signal, features, aggregate, grad_pre)
    outs = [jax.ShapeDtypeStruct((half_rows(wide), outw), F32)] * 2
    outs += [jax.ShapeDtypeStruct((BLK + 16, width), BF16)] * wide
    return pl.pallas_call(
        partial(grads_kernel, wide=wide),
        grid_spec=pltpu.PrefetchScalarGridSpec(
            num_scalar_prefetch=3,
            grid=(1,),
            in_specs=[whole(x) for x in ins],
            out_specs=[whole(x) for x in outs],
        ),
        out_shape=outs,
        compiler_params=params(),
        cost_estimate=cost(8 * rows * width * width, 16 * rows * width),
        name="grads",
    )(asked, row, valid, *ins)


def pack_kernel(mine_ref, come_ref, *refs, wide):
    pushed_refs, msg_refs = refs[:wide], refs[wide:]
    here = lax.axis_index("wide")
    piece = mine_ref.shape[0] // wide
    head = BLK + 16
    for k in range(wide):
        peer = target(here, k, wide)
        rows = pl.ds(pl.multiple_of(peer * piece, 16), piece)
        total = mine_ref[rows, :] + come_ref[rows, :]
        high = total.astype(BF16)
        low = (total - high.astype(F32)).astype(BF16)
        msg_refs[k][pl.ds(0, head), :] = pushed_refs[k][...]
        for j, x in enumerate((high[:, :BLK], high[:, BLK:], low[:, :BLK], low[:, BLK:])):
            msg_refs[k][pl.ds(head + j * piece, piece), :] = x


def pack(mine, come, pushed):
    wide = len(pushed)

    def whole(x):
        return pl.BlockSpec(x.shape, lambda i: (0,) * len(x.shape))

    ins = (mine, come, *pushed)
    tall = BLK + 16 + mine.shape[0] // wide * 4
    outs = [jax.ShapeDtypeStruct((tall, pushed[0].shape[1]), BF16)] * wide
    return pl.pallas_call(
        partial(pack_kernel, wide=wide),
        grid=(1,),
        in_specs=[whole(x) for x in ins],
        out_specs=[whole(x) for x in outs],
        out_shape=outs,
        compiler_params=params(),
        cost_estimate=cost(4 * mine.size, 20 * mine.size),
        name="pack",
    )(*ins)


def piece_sum_kernel(*refs):
    arrived, out_ref = refs[:-1], refs[-1]
    piece = out_ref.shape[0]
    head = BLK + 16
    for side in range(2):
        part = [
            a[pl.ds(head + side * piece, piece), :].astype(F32)
            + a[pl.ds(head + (side + 2) * piece, piece), :].astype(F32)
            for a in arrived
        ]
        out_ref[:, pl.ds(side * BLK, BLK)] = tree_sum(part)


def piece_sum(arrived):
    def whole(x):
        return pl.BlockSpec(x.shape, lambda i: (0,) * len(x.shape))

    piece = (arrived[0].shape[0] - BLK - 16) // 4
    out = jax.ShapeDtypeStruct((piece, 2 * BLK), F32)
    return pl.pallas_call(
        piece_sum_kernel,
        grid=(1,),
        in_specs=[whole(x) for x in arrived],
        out_specs=whole(out),
        out_shape=out,
        compiler_params=params(),
        cost_estimate=cost(arrived[0].size * len(arrived), 2 * arrived[0].size * len(arrived)),
        name="piece_sum",
    )(*arrived)


def half_kernel(*refs, factor):
    pieces, out_ref = refs[:-1], refs[-1]
    wide, piece = len(pieces), pieces[0].shape[0]
    here = lax.axis_index("wide")
    for k in range(wide):
        at = pl.ds(pl.multiple_of(source(here, k, wide) * piece, 16), piece)
        out_ref[at, :] = pieces[k][...] * factor


def half(pieces, factor):
    def whole(x):
        return pl.BlockSpec(x.shape, lambda i: (0, 0))

    out = jax.ShapeDtypeStruct((pieces[0].shape[0] * len(pieces), pieces[0].shape[1]), F32)
    return pl.pallas_call(
        partial(half_kernel, factor=factor),
        grid=(1,),
        in_specs=[whole(x) for x in pieces],
        out_specs=whole(out),
        out_shape=out,
        compiler_params=params(),
        cost_estimate=cost(out.size, 8 * out.size),
        name="half",
    )(*pieces)


def finish_kernel(total_ref, paired_ref, self_ref, neigh_ref, bias_ref):
    first = lax.rem(lax.axis_index("narrow"), 2) == 0
    total, paired = total_ref[pl.ds(0, BLK), :], paired_ref[pl.ds(0, BLK), :]
    self_ref[...] = jnp.where(first, total, paired)
    neigh_ref[...] = jnp.where(first, paired, total)
    at = pl.ds(BLK, 8)
    bias_ref[...] = jnp.where(first, total_ref[at, :], paired_ref[at, :])[:1]


def finish(total, paired):
    def whole(x):
        return pl.BlockSpec(x.shape, lambda i, *s: (0, 0))

    outs = [jax.ShapeDtypeStruct((r, 2 * BLK), F32) for r in (BLK, BLK, 1)]
    return pl.pallas_call(
        finish_kernel,
        grid=(1,),
        in_specs=[whole(total), whole(paired)],
        out_specs=[whole(x) for x in outs],
        out_shape=outs,
        compiler_params=params(),
        cost_estimate=cost(4 * total.size, 16 * total.size),
        name="finish",
    )(total, paired)


def base_kernel(gp_ref, wself_ref, keep_ref, *refs, parts):
    come, arrived, out_ref = refs[:parts], refs[parts:-1], refs[-1]
    tall = 4 * BLK
    for i in range(out_ref.shape[0] // tall):
        rows = pl.ds(i * tall, tall)
        out_ref[rows, :] = mm(gp_ref[rows, :], wself_ref[...], 1, 1) + keep_ref[rows, :].astype(F32)
    tall = come[0].shape[0]
    for j, part in enumerate(come):
        out_ref[pl.ds(j * tall, tall), :] += part[...].astype(F32)
    line = lax.broadcasted_iota(jnp.int32, (16, BLK), 0)
    for a in arrived:
        index = jnp.max(jnp.where(line == 0, a[pl.ds(BLK, 16), :].astype(F32), 0.0))
        at = pl.ds(pl.multiple_of(index.astype(jnp.int32) * BLK, BLK), BLK)
        out_ref[at, :] += a[pl.ds(0, BLK), :].astype(F32)


def base(grad_pre, w_self, keeps, come, arrived):
    count, rows, width = keeps.shape
    slab = pl.BlockSpec((None, rows, width), lambda i: (count - 1, 0, 0))
    head = pl.BlockSpec((BLK + 16, width), lambda i: (0, 0))
    out = jax.ShapeDtypeStruct((rows, width), F32)
    return pl.pallas_call(
        partial(base_kernel, parts=len(come)),
        grid=(1,),
        in_specs=[spec(grad_pre), spec(w_self), slab]
        + [spec(x) for x in come]
        + [head] * len(arrived),
        out_specs=spec(out),
        out_shape=out,
        compiler_params=params(),
        cost_estimate=cost(4 * rows * width * width, 12 * rows * width),
        name="base",
    )(grad_pre, w_self, keeps, *come, *arrived)


def joined_kernel(*refs):
    total = refs[0][...].astype(F32)
    for ref in refs[1:-1]:
        total = total + ref[...].astype(F32)
    refs[-1][...] = total.astype(BF16)


def joined(j, got, keeps, come, s):
    _, rows, width = keeps.shape
    tall = rows // SUM_CHUNKS
    keep = pl.BlockSpec((None, tall, width), lambda i: (s, j, 0))
    part = pl.BlockSpec((tall, width), lambda i: (j, 0))
    more = () if got is None else (got,)
    out = jax.ShapeDtypeStruct((tall, width), BF16)
    if len(come) > 1:
        per = len(come) // SUM_CHUNKS
        assert per == 1
        come, part = [come[j]], spec(come[j])
    return pl.pallas_call(
        joined_kernel,
        grid=(1,),
        in_specs=[spec(x) for x in more] + [keep, part],
        out_specs=spec(out),
        out_shape=out,
        compiler_params=params(),
        cost_estimate=cost(3 * tall * width, 8 * tall * width),
        name=f"joined{s}_{j}",
    )(*more, keeps, *come)


def last_kernel(rest_ref, *refs):
    got, out_ref = refs[:-1], refs[-1]
    tall = got[0].shape[0]
    for j, ref in enumerate(got):
        rows = pl.ds(j * tall, tall)
        out_ref[rows, :] = rest_ref[rows, :] + ref[...].astype(F32)


def last(rest, got):
    def whole(x):
        return pl.BlockSpec(x.shape, lambda i: (0, 0))

    return pl.pallas_call(
        last_kernel,
        grid=(1,),
        in_specs=[whole(x) for x in (rest, *got)],
        out_specs=whole(rest),
        out_shape=jax.ShapeDtypeStruct(rest.shape, F32),
        compiler_params=params(),
        cost_estimate=cost(rest.size, 10 * rest.size),
        name="last",
    )(rest, *got)


def power(size):
    return size & (size - 1) == 0


def target(i, k, size):
    return i ^ k if power(size) else lax.rem(i + k, size)


def source(i, k, size):
    return i ^ k if power(size) else lax.rem(i + size - k, size)


def to_peer(x, axis, k):
    size = lax.axis_size(axis)
    return lax.ppermute(x, axis, [(i, i ^ k if power(size) else (i + k) % size) for i in range(size)])


def back_to(x, axis, k):
    size = lax.axis_size(axis)
    return to_peer(x, axis, k if power(size) else size - k)


def tree_sum(parts):
    while len(parts) > 1:
        pairs = [a + b for a, b in zip(parts[::2], parts[1::2])]
        parts = pairs + parts[len(pairs) * 2 :]
    return parts[0]


def shards(
    features,
    band_tiles,
    band_cols,
    off_tiles,
    req_block,
    req_row,
    req_valid,
    weight_self,
    weight_neigh,
    bias_term,
    cotangent,
):
    row_count, width = features.shape
    n = lax.axis_size("narrow")
    wide = lax.axis_size("wide")
    steps = n // 2
    fold = fold_of(steps)
    after = {a: b for a, b in zip(fold, fold[1:] + fold[:1])}

    def onward(x):
        return lax.ppermute(x, "narrow", [(i, after[i // 2] * 2 + i % 2) for i in range(n)])

    def swap(x):
        return to_peer(x, "narrow", 1)

    cols = band_cols.T
    asked, row, valid = req_block[0], req_row[0], req_valid[0]
    def tie(*xs):
        return lax.optimization_barrier(xs)

    def cut(x):
        tall = row_count // CHUNKS
        return [x] if CHUNKS == 1 else [lax.slice_in_dim(x, j * tall, (j + 1) * tall) for j in range(CHUNKS)]

    tiles = band_tiles
    slabs, pairs = [cut(features)], []
    asked_of_me = [asked] + [to_peer(asked, "wide", k) for k in range(1, wide)]
    sums = ()
    for s in range(1, steps):
        following = [onward(x) for x in slabs[-1]]
        pairs.append([swap(features)] if s == 1 else [swap(x) for x in slabs[-1]])
        off = (row, valid, off_tiles, fetched) if s == steps - 1 else ()
        sums = pull(cols, tiles, slabs[-1], pairs[-1], sums, s - 1, off)
        at = 0 if s == 1 else -1
        following[at], *sums = tie(following[at], *sums)
        if s == 1:
            following[-1], *asked_of_me = tie(following[-1], *asked_of_me)
            served = serve(asked_of_me, features)
            fetched = [served[0]] + [back_to(served[k], "wide", k) for k in range(1, wide)]
        elif s == 2:
            following[-1], *fetched = tie(following[-1], *fetched)
        slabs.append(following)
        if s == steps - 2:
            halved = halve(tiles)
            halved, *sums = tie(halved, *sums)
    early = [swap(x) for x in slabs[-1][:-1]]
    slabs[-1][-1], *early = tie(slabs[-1][-1], *early)
    pairs.append([*early, swap(slabs[-1][-1])])
    layer_out, grad_pre, aggregate, signal, keep, send = middle(
        cols, halved, cotangent, sums, features, weight_self, weight_neigh,
        bias_term.reshape(1, -1), slabs[-1], pairs[-1], steps,
    )

    come = swap(send)
    keep2, send2 = push(cols, signal, halved, (2 % steps,))
    mine, other, *pushed = grads(
        asked, row, valid, off_tiles, signal, features, aggregate, grad_pre
    )
    come2 = [swap(x) for x in send2]
    come, mine, other, keep2, *more = tie(come, mine, other, keep2, *come2, *pushed)
    come2, pushed = more[: len(come2)], more[len(come2) :]
    each = range(SUM_CHUNKS)
    got = [onward(joined(j, None, keep[None], [come], 0)) for j in each]
    packed = pack(mine, swap(other), pushed)
    arrived = [packed[0]] + [to_peer(packed[k], "wide", k) for k in range(1, wide)]
    total = piece_sum(arrived)
    if not power(steps):
        total = lax.psum(total, "narrow", axis_index_groups=[list(range(c, n, 2)) for c in (0, 1)])
    later = tuple((s + 3) % steps for s in range(steps - 2))
    for s in range(steps - 2):
        if s == 0:
            got[0], _ = tie(got[0], total)
            if power(steps):
                total = tree_sum([total] + [to_peer(total, "narrow", 2 * k) for k in range(1, steps)])
        elif s == 1:
            got[0], total = tie(got[0], total)
            pieces = [total] + [to_peer(total, "wide", k) for k in range(1, wide)]
        if s == 0:
            got[0], signal = tie(got[0], signal)
            going = [joined(j, got[j], keep2, come2, 0) for j in each]
            keeps, sends = push(cols, signal, halved, later)
            comes = [swap(x) for x in sends]
            rest = base(grad_pre, weight_self, keeps, comes[-PARTS:], arrived)
        else:
            mid = comes[(s - 1) * PARTS : s * PARTS]
            going = [joined(j, got[j], keeps, mid, s - 1) for j in each]
        got = [onward(x) for x in going]
    got[0], rest, *pieces = tie(got[0], rest, *pieces)
    whole = half(pieces, (wide * n * row_count) ** (-0.5))
    grad_self, grad_neigh, grad_bias = finish(whole, swap(whole))
    got[-1], grad_self, grad_neigh, grad_bias = tie(got[-1], grad_self, grad_neigh, grad_bias)
    grad_features = last(rest, got)
    return layer_out, grad_features, grad_self, grad_neigh, grad_bias.reshape(-1)


def solution(mesh):
    both = ("wide", "narrow")
    placed = (
        P(both, None),
        P(both, None, None, None),
        P(both, None),
        P(both, None, None, None),
        P(both, None),
        P(both, None),
        P(both, None),
        P(),
        P(),
        P(),
        P(both, None),
    )
    return jax.shard_map(
        shards,
        mesh=mesh,
        in_specs=placed,
        out_specs=(P(both, None), P(both, None), P(), P(), P()),
        check_vma=False,
    )
```

```python
from functools import partial

import jax
import jax.numpy as jnp
from jax import lax
from jax.experimental import pallas as pl
from jax.experimental.pallas import tpu as pltpu
from jax.sharding import PartitionSpec as P

F32 = jnp.float32
BF16 = jnp.bfloat16
BLK = 128
ROWS_PER = 4
CHUNKS = 2
PARTS = 2
SUM_CHUNKS = 2
VMEM = 28 * 1024 * 1024


def mm(a, b, lhs=1, rhs=0):
    return lax.dot_general(a, b, (((lhs,), (rhs,)), ((), ())), preferred_element_type=F32)


def params():
    return pltpu.CompilerParams(vmem_limit_bytes=VMEM)


def cost(flops, nbytes, trans=0):
    return pl.CostEstimate(flops=flops, bytes_accessed=nbytes, transcendentals=trans)


def fold_of(steps):
    return [0] + list(range(1, steps, 2)) + list(range(2, steps, 2))[::-1]


class Place:
    def __init__(self, n):
        me = lax.axis_index("narrow")
        self.core, self.chip, self.steps = lax.rem(me, 2), lax.div(me, 2), n // 2

    def at(self, s):
        fold = fold_of(self.steps)
        found = jnp.int32(0)
        for z in range(self.steps):
            found = jnp.where(self.chip == z, fold[(fold.index(z) - s) % self.steps], found)
        return found


def block(ref, index):
    return ref[pl.ds(pl.multiple_of(index * BLK, BLK), BLK), :]


def tile_reads(tiles_ref, buffer, sems, chip):
    count = buffer.shape[0] // ROWS_PER
    reads = []
    for q in range(count):
        rows = pl.ds(q * ROWS_PER, ROWS_PER)
        reads.append(
            pltpu.make_async_copy(
                tiles_ref.at[rows, pl.ds(chip * 2, 2)], buffer.at[rows], sems.at[q]
            )
        )
    for r in reads:
        r.start()
    return reads


def pair_sum(core, cols, pair, slabs_ref, g, n, chip, base=0):
    own = block(slabs_ref.at[0], cols[chip * 2 + core, g])
    sib = block(slabs_ref.at[1], cols[chip * 2 + 1 - core, g])
    mine, other = pair[g, base + core].astype(F32), pair[g, base + 1 - core].astype(F32)
    return mm(mine.astype(BF16), own) + mm(other.astype(BF16), sib), mine + other


def lay_out(parts, slabs_ref):
    at = 0
    for part in parts:
        half, row = divmod(at, slabs_ref.shape[1])
        slabs_ref[half, pl.ds(row, part.shape[0]), :] = part[...]
        at += part.shape[0]


def spec(x):
    return pl.BlockSpec(x.shape, lambda *i: (0,) * len(x.shape))


def in_hbm():
    return pl.BlockSpec(memory_space=pltpu.HBM)


def halve_kernel(t_ref, out_ref):
    out_ref[...] = t_ref[...].astype(F32).astype(BF16)


def halve(tiles):
    g, n = tiles.shape[:2]
    one = pl.BlockSpec((1, n, BLK, BLK), lambda i: (i, 0, 0, 0))
    return pl.pallas_call(
        halve_kernel,
        grid=(g,),
        in_specs=[one],
        out_specs=one,
        out_shape=jax.ShapeDtypeStruct(tiles.shape, BF16),
        compiler_params=params(),
        cost_estimate=cost(tiles.size, 6 * tiles.size),
        name="halve",
    )(tiles)


def pull_kernel(cols, *refs, n, step, chunks, wide):
    refs = list(refs)
    if wide:
        row, valid = refs[:2]
        refs = refs[2:]
    tiles_ref, parts = refs[0], refs[1 : 1 + chunks]
    refs = refs[1 + chunks :]
    if step:
        acc_in, counts_in = refs[:2]
        refs = refs[2:]
    if wide:
        off_ref, fetched = refs[0], refs[1 : 1 + wide]
        refs = refs[1 + wide :]
        here = lax.axis_index("wide")
    acc_ref, counts_ref, slabs_ref, pair, sems = refs[:5]
    here_now = Place(n)
    core, chip = here_now.core, here_now.at(step)
    reads = tile_reads(tiles_ref, pair, sems, chip)
    lay_out(parts, slabs_ref)
    for q, r in enumerate(reads):
        r.wait()
        for g in range(q * ROWS_PER, (q + 1) * ROWS_PER):
            rows = pl.ds(g * BLK, BLK)
            part, count = pair_sum(core, cols, pair, slabs_ref, g, n, chip)
            acc_ref[rows, :] = acc_in[rows, :] + part if step else part
            counts_ref[rows, :] = counts_in[rows, :] + count if step else count
    if wide:
        for k in range(wide):
            src = target(here, k, wide)
            mask = (off_ref[0, src] * valid[src]).astype(F32)
            at = pl.ds(pl.multiple_of(row[src] * BLK, BLK), BLK)
            acc_ref[at, :] += mm(mask.astype(BF16), fetched[k][...])
            counts_ref[at, :] += mask


def pull(cols, tiles, own, sib, sums, step, off=()):
    g, n = tiles.shape[:2]
    width = own[0].shape[1]
    rows = g * BLK
    wide = 0
    scalars, ins = [], [*own, *sib, *sums]
    specs = [in_hbm()] + [spec(x) for x in ins]
    if off:
        *scalars, off_tiles, fetched = off
        wide = len(fetched)
        ins += [off_tiles, *fetched]
        specs += [spec(x) for x in (off_tiles, *fetched)]
    out = jax.ShapeDtypeStruct((rows, width), F32)
    return pl.pallas_call(
        partial(pull_kernel, n=n, step=step, chunks=len(own) + len(sib), wide=wide),
        grid_spec=pltpu.PrefetchScalarGridSpec(
            num_scalar_prefetch=1 + len(scalars),
            grid=(1,),
            in_specs=specs,
            out_specs=[spec(out)] * 2,
            scratch_shapes=[
                pltpu.VMEM((2, rows, width), BF16),
                pltpu.VMEM((g, 2, BLK, BLK), jnp.int32),
                pltpu.SemaphoreType.DMA((g // ROWS_PER,)),
            ],
        ),
        out_shape=[out] * 2,
        compiler_params=params(),
        cost_estimate=cost(4 * rows * BLK * width, 12 * rows * width),
        name=f"pull{step}",
    )(cols, *scalars, tiles, *ins)


def serve_kernel(*refs, wide):
    asked, feat_ref, outs = refs[:wide], refs[wide], refs[wide + 1 :]
    here = lax.axis_index("wide")
    for k in range(wide):
        outs[k][...] = block(feat_ref, asked[k][here])


def serve(asked, features):
    wide = len(asked)
    out = jax.ShapeDtypeStruct((BLK, features.shape[1]), features.dtype)
    return pl.pallas_call(
        partial(serve_kernel, wide=wide),
        grid_spec=pltpu.PrefetchScalarGridSpec(
            num_scalar_prefetch=wide,
            grid=(1,),
            in_specs=[spec(features)],
            out_specs=[spec(out)] * wide,
        ),
        out_shape=[out] * wide,
        compiler_params=params(),
        cost_estimate=cost(0, 4 * features.size),
        name="serve",
    )(*asked, features)


def place(cols, tiles_ref, signal_rows, place_ref, g, core, chip, n):
    for j in range(2):
        which = core if j == 0 else 1 - core
        at = pl.ds(pl.multiple_of(cols[chip * 2 + which, g] * BLK, BLK), BLK)
        place_ref[j, at, :] += mm(tiles_ref[g, chip * 2 + which], signal_rows, 0, 0)


def middle_kernel(
    cols, tiles_ref, cot_ref, acc_ref, counts_ref, feat_ref, wself_ref, wneigh_ref, bias_ref,
    *refs, n, steps, chunks,
):
    parts, refs = refs[: 2 * chunks], refs[2 * chunks :]
    out_hbm, gp_ref, agg_ref, sig_ref, keep_ref, send_ref = refs[:6]
    place_ref, slabs_ref, out, out_sems = refs[6:]
    place_now = Place(n)
    core, last, first = place_now.core, place_now.at(steps - 1), place_now.at(1)
    tall = ROWS_PER * BLK
    count = feat_ref.shape[0] // tall

    def rows_of(q):
        return pl.ds(q * tall, tall)

    writes = [
        pltpu.make_async_copy(out.at[rows_of(q)], out_hbm.at[rows_of(q)], out_sems.at[q])
        for q in range(count)
    ]
    place_ref[...] = jnp.zeros_like(place_ref)
    lay_out(parts, slabs_ref)
    ones = jnp.ones((BLK, BLK), BF16)
    slope = 0.7978845608028654
    for q in range(count):
        rows = rows_of(q)
        both = [
            pair_sum(core, cols, tiles_ref, slabs_ref, g, n, last, last * 2)
            for g in range(q * ROWS_PER, (q + 1) * ROWS_PER)
        ]
        gathered = acc_ref[rows, :] + jnp.concatenate([b[0] for b in both], axis=0)
        counts = counts_ref[rows, :] + jnp.concatenate([b[1] for b in both], axis=0)
        inverse = 1.0 / (mm(counts.astype(BF16), ones) + 1.0)
        aggregate = (gathered * inverse).astype(BF16)
        agg_ref[rows, :] = aggregate
        pre = mm(feat_ref[rows, :], wself_ref[...]) + mm(aggregate, wneigh_ref[...])
        pre = pre + bias_ref[...].astype(F32)
        square = pre * pre
        bent = jnp.tanh(slope * (pre + 0.044715 * (square * pre)))
        half = 0.5 * (1.0 + bent)
        out[rows, :] = (pre * half).astype(BF16)
        writes[q].start()
        deriv = half + (0.5 * pre) * (1.0 - bent * bent) * (
            slope + (3 * 0.044715 * slope) * square
        )
        grad_pre = (cot_ref[rows, :].astype(F32) * deriv).astype(BF16)
        gp_ref[rows, :] = grad_pre
        signal = (mm(grad_pre, wneigh_ref[...], 1, 1) * inverse).astype(BF16)
        sig_ref[rows, :] = signal
        for b in range(ROWS_PER):
            rows_b = signal[b * BLK : (b + 1) * BLK]
            place(cols, tiles_ref, rows_b, place_ref, q * ROWS_PER + b, core, first, n)
    keep_ref[...] = place_ref[0].astype(BF16)
    send_ref[...] = place_ref[1].astype(BF16)
    for w in writes:
        w.wait()


def middle(cols, tiles, cot, sums, features, w_self, w_neigh, bias, own, sib, steps):
    g, n = tiles.shape[:2]
    rows, width = features.shape
    outw = w_self.shape[1]
    count = g // ROWS_PER

    def shape(c):
        return jax.ShapeDtypeStruct((rows, c), BF16)

    ins = (*sums, features, w_self, w_neigh, bias, *own, *sib)
    outs = [shape(outw), shape(outw), shape(width), shape(width), shape(width), shape(width)]
    return pl.pallas_call(
        partial(middle_kernel, n=n, steps=steps, chunks=len(own)),
        grid_spec=pltpu.PrefetchScalarGridSpec(
            num_scalar_prefetch=1,
            grid=(1,),
            in_specs=[spec(x) for x in (tiles, cot, *ins)],
            out_specs=[in_hbm()] + [spec(x) for x in outs[1:]],
            scratch_shapes=[
                pltpu.VMEM((2, rows, width), F32),
                pltpu.VMEM((2, rows, width), BF16),
                pltpu.VMEM((rows, outw), BF16),
                pltpu.SemaphoreType.DMA((count,)),
            ],
        ),
        out_shape=outs,
        compiler_params=params(),
        cost_estimate=cost(
            8 * rows * BLK * width + 6 * rows * width * outw, 30 * rows * width, rows * outw
        ),
        name="middle",
    )(cols, tiles, cot, *ins)


def push_kernel(cols, tiles_ref, sig_ref, keep_ref, *refs, n, which):
    *send_refs, place_ref = refs
    now = Place(n)
    parts = len(send_refs) // len(which)
    tall = send_refs[0].shape[0]
    for p, s in enumerate(which):
        place_ref[...] = jnp.zeros_like(place_ref)
        for g in range(tiles_ref.shape[0]):
            rows = sig_ref[g * BLK : (g + 1) * BLK, :]
            place(cols, tiles_ref, rows, place_ref, g, now.core, now.at(s), n)
        keep_ref[p] = place_ref[0].astype(BF16)
        for j in range(parts):
            send_refs[p * parts + j][...] = place_ref[1, pl.ds(j * tall, tall), :].astype(BF16)


def push(cols, signal, tiles, which):
    g, n = tiles.shape[:2]
    rows, width = signal.shape
    count = len(which)
    outs = [jax.ShapeDtypeStruct((count, rows, width), BF16)]
    outs += [jax.ShapeDtypeStruct((rows // PARTS, width), BF16)] * (count * PARTS)
    keeps, *sends = pl.pallas_call(
        partial(push_kernel, n=n, which=which),
        grid_spec=pltpu.PrefetchScalarGridSpec(
            num_scalar_prefetch=1,
            grid=(1,),
            in_specs=[spec(tiles), spec(signal)],
            out_specs=[spec(x) for x in outs],
            scratch_shapes=[pltpu.VMEM((2, rows, width), F32)],
        ),
        out_shape=outs,
        compiler_params=params(),
        cost_estimate=cost(4 * count * rows * BLK * width, 8 * count * rows * width),
        name="push",
    )(cols, tiles, signal)
    return keeps, sends


def half_rows(wide):
    step = 16 * wide
    return (BLK + 1 + step - 1) // step * step


def grads_kernel(
    asked, row, valid, off_ref, sig_ref, feat_ref, agg_ref, gp_ref,
    mine_ref, other_ref, *pushed_refs, wide,
):
    here = lax.axis_index("wide")
    tall = 4 * BLK
    dself = dneigh = dbias = None
    for i in range(feat_ref.shape[0] // tall):
        rows = pl.ds(i * tall, tall)
        gp = gp_ref[rows, :]
        a = mm(feat_ref[rows, :], gp, 0, 0)
        b = mm(agg_ref[rows, :], gp, 0, 0)
        c = jnp.sum(gp.astype(F32), axis=0, keepdims=True)
        dself, dneigh, dbias = (a, b, c) if i == 0 else (dself + a, dneigh + b, dbias + c)
    first = lax.rem(lax.axis_index("narrow"), 2) == 0
    mine_ref[pl.ds(0, BLK), :] = jnp.where(first, dself, dneigh)
    other_ref[pl.ds(0, BLK), :] = jnp.where(first, dneigh, dself)
    spare = mine_ref.shape[0] - BLK
    mine_ref[pl.ds(BLK, spare), :] = jnp.broadcast_to(dbias, (spare, dbias.shape[1]))
    other_ref[pl.ds(BLK, spare), :] = jnp.broadcast_to(dbias, (spare, dbias.shape[1]))
    for k in range(wide):
        peer = target(here, k, wide)
        mask = (off_ref[0, peer] * valid[peer]).astype(F32).astype(BF16)
        at = pl.ds(pl.multiple_of(row[peer] * BLK, BLK), BLK)
        ref = pushed_refs[k]
        ref[pl.ds(0, BLK), :] = mm(mask, sig_ref[at, :], 0, 0).astype(BF16)
        ref[pl.ds(BLK, 16), :] = jnp.full((16, BLK), asked[peer], jnp.int32).astype(F32).astype(BF16)


def grads(asked, row, valid, off_tiles, signal, features, aggregate, grad_pre):
    wide = off_tiles.shape[1]
    rows, width = features.shape
    outw = grad_pre.shape[1]

    def whole(x):
        return pl.BlockSpec(x.shape, lambda i, *s: (0,) * len(x.shape))

    ins = (off_tiles, signal, features, aggregate, grad_pre)
    outs = [jax.ShapeDtypeStruct((half_rows(wide), outw), F32)] * 2
    outs += [jax.ShapeDtypeStruct((BLK + 16, width), BF16)] * wide
    return pl.pallas_call(
        partial(grads_kernel, wide=wide),
        grid_spec=pltpu.PrefetchScalarGridSpec(
            num_scalar_prefetch=3,
            grid=(1,),
            in_specs=[whole(x) for x in ins],
            out_specs=[whole(x) for x in outs],
        ),
        out_shape=outs,
        compiler_params=params(),
        cost_estimate=cost(8 * rows * width * width, 16 * rows * width),
        name="grads",
    )(asked, row, valid, *ins)


def pack_kernel(mine_ref, come_ref, *refs, wide):
    pushed_refs, msg_refs = refs[:wide], refs[wide:]
    here = lax.axis_index("wide")
    piece = mine_ref.shape[0] // wide
    head = BLK + 16
    for k in range(wide):
        peer = target(here, k, wide)
        rows = pl.ds(pl.multiple_of(peer * piece, 16), piece)
        total = mine_ref[rows, :] + come_ref[rows, :]
        high = total.astype(BF16)
        low = (total - high.astype(F32)).astype(BF16)
        msg_refs[k][pl.ds(0, head), :] = pushed_refs[k][...]
        for j, x in enumerate((high[:, :BLK], high[:, BLK:], low[:, :BLK], low[:, BLK:])):
            msg_refs[k][pl.ds(head + j * piece, piece), :] = x


def pack(mine, come, pushed):
    wide = len(pushed)

    def whole(x):
        return pl.BlockSpec(x.shape, lambda i: (0,) * len(x.shape))

    ins = (mine, come, *pushed)
    tall = BLK + 16 + mine.shape[0] // wide * 4
    outs = [jax.ShapeDtypeStruct((tall, pushed[0].shape[1]), BF16)] * wide
    return pl.pallas_call(
        partial(pack_kernel, wide=wide),
        grid=(1,),
        in_specs=[whole(x) for x in ins],
        out_specs=[whole(x) for x in outs],
        out_shape=outs,
        compiler_params=params(),
        cost_estimate=cost(4 * mine.size, 20 * mine.size),
        name="pack",
    )(*ins)


def piece_sum_kernel(*refs):
    arrived, out_ref = refs[:-1], refs[-1]
    piece = out_ref.shape[0]
    head = BLK + 16
    for side in range(2):
        part = [
            a[pl.ds(head + side * piece, piece), :].astype(F32)
            + a[pl.ds(head + (side + 2) * piece, piece), :].astype(F32)
            for a in arrived
        ]
        out_ref[:, pl.ds(side * BLK, BLK)] = tree_sum(part)


def piece_sum(arrived):
    def whole(x):
        return pl.BlockSpec(x.shape, lambda i: (0,) * len(x.shape))

    piece = (arrived[0].shape[0] - BLK - 16) // 4
    out = jax.ShapeDtypeStruct((piece, 2 * BLK), F32)
    return pl.pallas_call(
        piece_sum_kernel,
        grid=(1,),
        in_specs=[whole(x) for x in arrived],
        out_specs=whole(out),
        out_shape=out,
        compiler_params=params(),
        cost_estimate=cost(arrived[0].size * len(arrived), 2 * arrived[0].size * len(arrived)),
        name="piece_sum",
    )(*arrived)


def half_kernel(*refs, factor):
    pieces, out_ref = refs[:-1], refs[-1]
    wide, piece = len(pieces), pieces[0].shape[0]
    here = lax.axis_index("wide")
    for k in range(wide):
        at = pl.ds(pl.multiple_of(source(here, k, wide) * piece, 16), piece)
        out_ref[at, :] = pieces[k][...] * factor


def half(pieces, factor):
    def whole(x):
        return pl.BlockSpec(x.shape, lambda i: (0, 0))

    out = jax.ShapeDtypeStruct((pieces[0].shape[0] * len(pieces), pieces[0].shape[1]), F32)
    return pl.pallas_call(
        partial(half_kernel, factor=factor),
        grid=(1,),
        in_specs=[whole(x) for x in pieces],
        out_specs=whole(out),
        out_shape=out,
        compiler_params=params(),
        cost_estimate=cost(out.size, 8 * out.size),
        name="half",
    )(*pieces)


def finish_kernel(total_ref, paired_ref, self_ref, neigh_ref, bias_ref):
    first = lax.rem(lax.axis_index("narrow"), 2) == 0
    total, paired = total_ref[pl.ds(0, BLK), :], paired_ref[pl.ds(0, BLK), :]
    self_ref[...] = jnp.where(first, total, paired)
    neigh_ref[...] = jnp.where(first, paired, total)
    at = pl.ds(BLK, 8)
    bias_ref[...] = jnp.where(first, total_ref[at, :], paired_ref[at, :])[:1]


def finish(total, paired):
    def whole(x):
        return pl.BlockSpec(x.shape, lambda i, *s: (0, 0))

    outs = [jax.ShapeDtypeStruct((r, 2 * BLK), F32) for r in (BLK, BLK, 1)]
    return pl.pallas_call(
        finish_kernel,
        grid=(1,),
        in_specs=[whole(total), whole(paired)],
        out_specs=[whole(x) for x in outs],
        out_shape=outs,
        compiler_params=params(),
        cost_estimate=cost(4 * total.size, 16 * total.size),
        name="finish",
    )(total, paired)


def base_kernel(gp_ref, wself_ref, keep_ref, *refs, parts):
    come, arrived, out_ref = refs[:parts], refs[parts:-1], refs[-1]
    tall = 4 * BLK
    for i in range(out_ref.shape[0] // tall):
        rows = pl.ds(i * tall, tall)
        out_ref[rows, :] = mm(gp_ref[rows, :], wself_ref[...], 1, 1) + keep_ref[rows, :].astype(F32)
    tall = come[0].shape[0]
    for j, part in enumerate(come):
        out_ref[pl.ds(j * tall, tall), :] += part[...].astype(F32)
    line = lax.broadcasted_iota(jnp.int32, (16, BLK), 0)
    for a in arrived:
        index = jnp.max(jnp.where(line == 0, a[pl.ds(BLK, 16), :].astype(F32), 0.0))
        at = pl.ds(pl.multiple_of(index.astype(jnp.int32) * BLK, BLK), BLK)
        out_ref[at, :] += a[pl.ds(0, BLK), :].astype(F32)


def base(grad_pre, w_self, keeps, come, arrived):
    count, rows, width = keeps.shape
    slab = pl.BlockSpec((None, rows, width), lambda i: (count - 1, 0, 0))
    head = pl.BlockSpec((BLK + 16, width), lambda i: (0, 0))
    out = jax.ShapeDtypeStruct((rows, width), F32)
    return pl.pallas_call(
        partial(base_kernel, parts=len(come)),
        grid=(1,),
        in_specs=[spec(grad_pre), spec(w_self), slab]
        + [spec(x) for x in come]
        + [head] * len(arrived),
        out_specs=spec(out),
        out_shape=out,
        compiler_params=params(),
        cost_estimate=cost(4 * rows * width * width, 12 * rows * width),
        name="base",
    )(grad_pre, w_self, keeps, *come, *arrived)


def joined_kernel(*refs):
    total = refs[0][...].astype(F32)
    for ref in refs[1:-1]:
        total = total + ref[...].astype(F32)
    refs[-1][...] = total.astype(BF16)


def joined(j, got, keeps, come, s):
    _, rows, width = keeps.shape
    tall = rows // SUM_CHUNKS
    keep = pl.BlockSpec((None, tall, width), lambda i: (s, j, 0))
    part = pl.BlockSpec((tall, width), lambda i: (j, 0))
    more = () if got is None else (got,)
    out = jax.ShapeDtypeStruct((tall, width), BF16)
    if len(come) > 1:
        per = len(come) // SUM_CHUNKS
        assert per == 1
        come, part = [come[j]], spec(come[j])
    return pl.pallas_call(
        joined_kernel,
        grid=(1,),
        in_specs=[spec(x) for x in more] + [keep, part],
        out_specs=spec(out),
        out_shape=out,
        compiler_params=params(),
        cost_estimate=cost(3 * tall * width, 8 * tall * width),
        name=f"joined{s}_{j}",
    )(*more, keeps, *come)


def last_kernel(rest_ref, *refs):
    got, out_ref = refs[:-1], refs[-1]
    tall = got[0].shape[0]
    for j, ref in enumerate(got):
        rows = pl.ds(j * tall, tall)
        out_ref[rows, :] = rest_ref[rows, :] + ref[...].astype(F32)


def last(rest, got):
    def whole(x):
        return pl.BlockSpec(x.shape, lambda i: (0, 0))

    return pl.pallas_call(
        last_kernel,
        grid=(1,),
        in_specs=[whole(x) for x in (rest, *got)],
        out_specs=whole(rest),
        out_shape=jax.ShapeDtypeStruct(rest.shape, F32),
        compiler_params=params(),
        cost_estimate=cost(rest.size, 10 * rest.size),
        name="last",
    )(rest, *got)


def power(size):
    return size & (size - 1) == 0


def target(i, k, size):
    return i ^ k if power(size) else lax.rem(i + k, size)


def source(i, k, size):
    return i ^ k if power(size) else lax.rem(i + size - k, size)


def to_peer(x, axis, k):
    size = lax.axis_size(axis)
    return lax.ppermute(x, axis, [(i, i ^ k if power(size) else (i + k) % size) for i in range(size)])


def back_to(x, axis, k):
    size = lax.axis_size(axis)
    return to_peer(x, axis, k if power(size) else size - k)


def tree_sum(parts):
    while len(parts) > 1:
        pairs = [a + b for a, b in zip(parts[::2], parts[1::2])]
        parts = pairs + parts[len(pairs) * 2 :]
    return parts[0]


def shards(
    features,
    band_tiles,
    band_cols,
    off_tiles,
    req_block,
    req_row,
    req_valid,
    weight_self,
    weight_neigh,
    bias_term,
    cotangent,
):
    row_count, width = features.shape
    n = lax.axis_size("narrow")
    wide = lax.axis_size("wide")
    steps = n // 2
    fold = fold_of(steps)
    after = {a: b for a, b in zip(fold, fold[1:] + fold[:1])}

    def onward(x):
        return lax.ppermute(x, "narrow", [(i, after[i // 2] * 2 + i % 2) for i in range(n)])

    def swap(x):
        return to_peer(x, "narrow", 1)

    cols = band_cols.T
    asked, row, valid = req_block[0], req_row[0], req_valid[0]
    def tie(*xs):
        return lax.optimization_barrier(xs)

    def cut(x):
        tall = row_count // CHUNKS
        return [x] if CHUNKS == 1 else [lax.slice_in_dim(x, j * tall, (j + 1) * tall) for j in range(CHUNKS)]

    tiles = band_tiles
    slabs, pairs = [cut(features)], []
    asked_of_me = [asked] + [to_peer(asked, "wide", k) for k in range(1, wide)]
    sums = ()
    for s in range(1, steps):
        following = [onward(x) for x in slabs[-1]]
        pairs.append([swap(features)] if s == 1 else [swap(x) for x in slabs[-1]])
        off = (row, valid, off_tiles, fetched) if s == steps - 1 else ()
        sums = pull(cols, tiles, slabs[-1], pairs[-1], sums, s - 1, off)
        at = 0 if s == 1 else -1
        following[at], *sums = tie(following[at], *sums)
        if s == 1:
            following[-1], *asked_of_me = tie(following[-1], *asked_of_me)
            served = serve(asked_of_me, features)
            fetched = [served[0]] + [back_to(served[k], "wide", k) for k in range(1, wide)]
        elif s == 2:
            following[-1], *fetched = tie(following[-1], *fetched)
        slabs.append(following)
        if s == steps - 2:
            halved = halve(tiles)
            halved, *sums = tie(halved, *sums)
    early = [swap(x) for x in slabs[-1][:-1]]
    slabs[-1][-1], *early = tie(slabs[-1][-1], *early)
    pairs.append([*early, swap(slabs[-1][-1])])
    layer_out, grad_pre, aggregate, signal, keep, send = middle(
        cols, halved, cotangent, sums, features, weight_self, weight_neigh,
        bias_term.reshape(1, -1), slabs[-1], pairs[-1], steps,
    )

    come = swap(send)
    keep2, send2 = push(cols, signal, halved, (2 % steps,))
    mine, other, *pushed = grads(
        asked, row, valid, off_tiles, signal, features, aggregate, grad_pre
    )
    come2 = [swap(x) for x in send2]
    come, mine, other, keep2, *more = tie(come, mine, other, keep2, *come2, *pushed)
    come2, pushed = more[: len(come2)], more[len(come2) :]
    each = range(SUM_CHUNKS)
    got = [onward(joined(j, None, keep[None], [come], 0)) for j in each]
    packed = pack(mine, swap(other), pushed)
    arrived = [packed[0]] + [to_peer(packed[k], "wide", k) for k in range(1, wide)]
    total = piece_sum(arrived)
    if not power(steps):
        total = lax.psum(total, "narrow", axis_index_groups=[list(range(c, n, 2)) for c in (0, 1)])
    later = tuple((s + 3) % steps for s in range(steps - 2))
    for s in range(steps - 2):
        if s == 0:
            got[0], _ = tie(got[0], total)
            if power(steps):
                total = tree_sum([total] + [to_peer(total, "narrow", 2 * k) for k in range(1, steps)])
        elif s == 1:
            got[0], total, *own = tie(got[0], total, *sends[-PARTS:])
            rest = base(grad_pre, weight_self, keeps, [swap(x) for x in own], arrived)
            pieces = [total] + [to_peer(total, "wide", k) for k in range(1, wide)]
        if s == 0:
            got[0], signal = tie(got[0], signal)
            going = [joined(j, got[j], keep2, come2, 0) for j in each]
            keeps, sends = push(cols, signal, halved, later)
            comes = [swap(x) for x in sends[:-PARTS]]
        else:
            mid = comes[(s - 1) * PARTS : s * PARTS]
            going = [joined(j, got[j], keeps, mid, s - 1) for j in each]
        got = [onward(x) for x in going]
    got[0], rest, *pieces = tie(got[0], rest, *pieces)
    whole = half(pieces, (wide * n * row_count) ** (-0.5))
    grad_self, grad_neigh, grad_bias = finish(whole, swap(whole))
    got[-1], grad_self, grad_neigh, grad_bias = tie(got[-1], grad_self, grad_neigh, grad_bias)
    grad_features = last(rest, got)
    return layer_out, grad_features, grad_self, grad_neigh, grad_bias.reshape(-1)


def solution(mesh):
    both = ("wide", "narrow")
    placed = (
        P(both, None),
        P(both, None, None, None),
        P(both, None),
        P(both, None, None, None),
        P(both, None),
        P(both, None),
        P(both, None),
        P(),
        P(),
        P(),
        P(both, None),
    )
    return jax.shard_map(
        shards,
        mesh=mesh,
        in_specs=placed,
        out_specs=(P(both, None), P(both, None), P(), P(), P()),
        check_vma=False,
    )
```
